32 devices in a mesh: dp: 2 (over y), node: 4 (over z), local: 4 (over x, core).
Axes of the slice: x: 2, y: 2, z: 4, core: 2. Of those that a mesh axis runs over, the one named last changes fastest.
Arguments:
- tokens: bfloat16 [512, 2048], P(('dp', 'node', 'local')), parts along dimension 0, may hold values from -6 to 6
- cotangent: bfloat16 [512, 2048], P(('dp', 'node', 'local')), parts along dimension 0, may hold values from -6 to 6
- expert_ids: int32 [512, 8], P(('dp', 'node', 'local')), parts along dimension 0, may hold values from 0 to 15, all different within a row; in each aligned block of 16 rows (0 to 15, 16 to 31, ...) at most 16 rows name the same one
- combine: float32 [512, 8], P(('dp', 'node', 'local')), parts along dimension 0, may hold values from 0.05 to 0.3
- w_gate_up: bfloat16 [16, 2048, 768], P(('node', 'local')), may hold values from -0.125 to 0.125
- w_down: bfloat16 [16, 384, 2048], P(('node', 'local')), may hold values from -0.3125 to 0.3125
Outputs:
- mixed: bfloat16 [512, 2048], P(('dp', 'node', 'local')), parts along dimension 0
- grad_tokens: bfloat16 [512, 2048], P(('dp', 'node', 'local')), parts along dimension 0
- grad_combine: float32 [512, 8], P(('dp', 'node', 'local')), parts along dimension 0
The draws below stay inside these ranges and needn't reach their ends.
There are 2 independent parts, one for each index of `dp`. The reference program is written for one: setup_inputs(seed, part) draws one part's arguments, and reference() takes and returns one part's arrays. A program takes and returns all parts, laid end to end along the dimension named above; an argument that names none is the same for every part. Nothing has to cross between parts.
Inputs may be any that keep to these rules, and one draw needn't show every extreme that they name: `expert_ids`: each row names 8 different experts. Among the rows of one device no expert is named more than 16 times, a bound that some block reaches.
All inputs are finite; a program needn't handle non-finite values.
Results may differ from the reference program's by a relative error of at most 0.012.
Values may be sent and summed in bfloat16 or wider, within the bound.
A program may use at most 64 MiB of HBM per device.

```python
import math
import jax
import jax.numpy as jnp
import numpy as np
from jax import lax

D = 2048
FF = 384
TOP = 8
TOK_DEV = 16
EXPERTS = 16
CAP = 16
TOKENS = 256
N_NODE = 4
N_LOCAL = 4


def levels(stream_key, shape, pieces, least, largest):
    def one(position, blocks):
        heights = jax.random.uniform(jax.random.fold_in(jax.random.fold_in(stream_key, 6), position), (blocks,), jnp.float32, least / len(pieces), largest / len(pieces))
        return jnp.repeat(jnp.exp(heights), shape[position] // blocks).reshape((-1,) + (1,) * (len(shape) - position - 1))

    factor_of = one(*pieces[0])
    for cut in pieces[1:]:
        factor_of = factor_of * one(*cut)
    return factor_of


def routed_block(key, own, number, rows, amount, top, limit, lean):
    ranking = jax.random.permutation(key, amount)
    crowded, common = shares(amount, rows * top, limit, lean, True), shares(amount, rows * top, limit, lean, False)
    places = jnp.arange(amount)

    def named(sizes, offset_by):
        used = int((sizes > 0).sum())
        fixed = max(1, used // 4)
        passed = fixed + (places - fixed + offset_by * (used - fixed)) % max(1, amount - fixed)
        return jnp.zeros((amount,), jnp.int32).at[ranking[jnp.where(places < fixed, places, passed)]].set(jnp.asarray(sizes, jnp.int32))

    sizes = jnp.where(number % 4 == 0, named(crowded, number // 4), named(common, number - number // 4 - 1))
    mixed = jax.random.permutation(jax.random.fold_in(own, 3), amount)
    donor, receiver = mixed[0:amount // 2 * 2:2], mixed[1:amount // 2 * 2:2]
    slack = jnp.minimum(sizes[donor] - 1, limit - sizes[receiver]) // 2
    slack = jnp.where((donor == ranking[0]) | (receiver == ranking[0]) | (sizes[receiver] == 0), 0, jnp.maximum(slack, 0))
    passed = jax.random.randint(jax.random.fold_in(own, 4), (amount // 2,), 0, 1 << 20) % (slack + 1)
    sizes = sizes.at[donor].add(-passed).at[receiver].add(passed)
    members = jnp.searchsorted(jnp.cumsum(sizes), jnp.arange(rows * top), side="right").astype(jnp.int32)
    listing = members.reshape(top, rows).T
    listing = listing[jax.random.permutation(jax.random.fold_in(own, 1), rows)]
    offset_by = jax.random.randint(jax.random.fold_in(own, 2), (rows, 1), 0, top)
    return jnp.take_along_axis(listing, (jnp.arange(top)[None, :] + offset_by) % top, axis=1)


def shares(count, total, reach, lean, full):
    loads = [(1 << 20) // math.isqrt(standing ** lean) + 1 for standing in range(1, count + 1)]
    largest = reach if full else min(reach, max(-(-total // count), total * loads[0] // sum(loads)))
    least = 1 if total - largest >= count - 1 else 0
    given, rest = [largest] + [least] * (count - 1), total - largest - least * (count - 1)
    while rest > 0:
        movable = [i for i in range(1, count) if given[i] < largest] or [i for i in range(1, count) if given[i] < reach]
        mass, left = sum([loads[i] for i in movable]), rest
        for i in movable:
            extra = min(reach - given[i], max(1, left * loads[i] // mass), rest)
            given[i] = given[i] + extra
            rest = rest - extra
    return np.array(given)


def gaussian(key, extent, scale, reach, shards=(), kind=jnp.bfloat16):
    drawn = jax.random.normal(key, extent, jnp.float32) * scale
    if len(shards) > 0:
        drawn = levels(key, extent, shards, -0.22, 0.18) * drawn
    return jnp.clip(drawn, min=-reach, max=reach).astype(kind)


def setup_inputs(seed: int = 0, part: int = 0) -> dict:
    key_list = jax.random.split(jax.random.key(seed), 7)
    own_keys = jax.random.split(jax.random.fold_in(key_list[6], part), 7)
    tokens = gaussian(own_keys[0], (TOKENS, D), 1.0, 6.0, ((0, 16),))
    cotangent = gaussian(own_keys[1], (TOKENS, D), 1.0, 6.0, ((0, 16),))
    expert_ids_keys = jax.random.split(jax.random.fold_in(own_keys[2], 1), TOKENS // TOK_DEV)
    expert_ids_turns = jax.random.permutation(jax.random.fold_in(own_keys[2], 3), TOKENS // TOK_DEV)
    expert_ids = jax.vmap(lambda own, number: routed_block(jax.random.fold_in(own_keys[2], 2), own, number, TOK_DEV, EXPERTS, TOP, CAP, 2))(expert_ids_keys, expert_ids_turns).reshape((TOKENS, TOP))
    combine = jnp.clip(0.05 + 0.25 * jax.random.uniform(own_keys[3], (TOKENS, TOP), jnp.float32) ** levels(own_keys[3], (TOKENS, TOP), ((0, 16),), -0.2, 0.2), 0.05, 0.3)
    w_gate_up = gaussian(key_list[4], (EXPERTS, D, 2 * FF), D ** -0.5, 0.125, ((0, 16),))
    w_down = gaussian(key_list[5], (EXPERTS, FF, D), FF ** -0.5, 0.3125, ((0, 16),))
    return dict(tokens=tokens, cotangent=cotangent, expert_ids=expert_ids, combine=combine, w_gate_up=w_gate_up, w_down=w_down)


def expert_forward(rows, w_gate_up, w_down):
    width = w_down.shape[0]
    projected = jnp.dot(rows, w_gate_up, preferred_element_type=jnp.float32)
    gate = projected[:, :width]
    upward = projected[:, width:]
    hidden = (gate * jax.nn.sigmoid(gate) * upward).astype(jnp.bfloat16)
    output = jnp.dot(hidden, w_down, preferred_element_type=jnp.float32).astype(jnp.bfloat16)
    return output, gate, upward


def expert_backward(grads, gate, upward, w_gate_up, w_down):
    grad_hidden = lax.dot_general(grads, w_down, (((1,), (1,)), ((), ())), preferred_element_type=jnp.float32)
    sigmoid = jax.nn.sigmoid(gate)
    grad_gate = grad_hidden * upward * sigmoid * (1.0 + gate * (1.0 - sigmoid))
    grad_up = grad_hidden * gate * sigmoid
    paired = jnp.concatenate([grad_gate, grad_up], axis=1).astype(jnp.bfloat16)
    back = lax.dot_general(paired, w_gate_up, (((1,), (1,)), ((), ())), preferred_element_type=jnp.float32)
    return back.astype(jnp.bfloat16)


def reference(tokens, cotangent, expert_ids, combine, w_gate_up, w_down):
    devices = N_NODE * N_LOCAL
    flat_ids = expert_ids.reshape(devices, TOK_DEV * TOP).astype(jnp.int32)
    onehot = (flat_ids[:, :, None] == jnp.arange(EXPERTS, dtype=jnp.int32)[None, None, :]).astype(jnp.int32)
    before = jnp.cumsum(onehot, axis=1).astype(jnp.int32) - onehot
    ranks = jnp.sum(before * onehot, axis=2).astype(jnp.int32)
    source = jnp.arange(devices, dtype=jnp.int32)[:, None]
    slots = (flat_ids * (devices * CAP) + source * CAP + ranks).reshape(-1).astype(jnp.int32)
    total = EXPERTS * devices * CAP
    weights = combine.reshape(-1)
    copies_x = jnp.repeat(tokens, TOP, axis=0)
    copies_g = (jnp.repeat(cotangent.astype(jnp.float32), TOP, axis=0) * weights[:, None]).astype(jnp.bfloat16)
    buffer_x = jnp.zeros((total, D), jnp.bfloat16).at[slots].set(copies_x).reshape(EXPERTS, devices * CAP, D)
    buffer_g = jnp.zeros((total, D), jnp.bfloat16).at[slots].set(copies_g).reshape(EXPERTS, devices * CAP, D)

    def per_expert(items):
        rows, grads, gate_up_one, down_one = items
        output, gate, upward = expert_forward(rows, gate_up_one, down_one)
        back = expert_backward(grads, gate, upward, gate_up_one, down_one)
        return output, back

    outputs, backs = lax.map(per_expert, (buffer_x, buffer_g, w_gate_up, w_down))
    picked = outputs.reshape(total, D)[slots].reshape(TOKENS, TOP, D).astype(jnp.float32)
    picked_back = backs.reshape(total, D)[slots].reshape(TOKENS, TOP, D).astype(jnp.float32)
    mixed = jnp.sum(combine[:, :, None] * picked, axis=1).astype(jnp.bfloat16)
    grad_tokens = jnp.sum(picked_back, axis=1).astype(jnp.bfloat16)
    grad_combine = jnp.sum(picked * cotangent.astype(jnp.float32)[:, None, :], axis=2)
    return mixed, grad_tokens, grad_combine
```

```python
import functools

import jax
import jax.numpy as jnp
from jax import lax
from jax.experimental import pallas as pl
from jax.experimental.pallas import tpu as pltpu
from jax.sharding import PartitionSpec as P

MESH = pl.DeviceIdType.MESH
LANES = 128
F32 = jnp.float32
BF16 = jnp.bfloat16


def expert_forward(rows, w_gate_up, w_down):
    width = w_down.shape[0]
    projected = jnp.dot(rows, w_gate_up, preferred_element_type=jnp.float32)
    gate = projected[:, :width]
    upward = projected[:, width:]
    hidden = (gate * jax.nn.sigmoid(gate) * upward).astype(jnp.bfloat16)
    output = jnp.dot(hidden, w_down, preferred_element_type=jnp.float32).astype(jnp.bfloat16)
    return (output, gate, upward)


def expert_backward(grads, gate, upward, w_gate_up, w_down):
    grad_hidden = lax.dot_general(
        grads, w_down, (((1,), (1,)), ((), ())), preferred_element_type=jnp.float32
    )
    sigmoid = jax.nn.sigmoid(gate)
    grad_gate = grad_hidden * upward * sigmoid * (1.0 + gate * (1.0 - sigmoid))
    grad_up = grad_hidden * gate * sigmoid
    paired = jnp.concatenate([grad_gate, grad_up], axis=1).astype(jnp.bfloat16)
    back = lax.dot_general(
        paired, w_gate_up, (((1,), (1,)), ((), ())), preferred_element_type=jnp.float32
    )
    return back.astype(jnp.bfloat16)


def node_tables(ids_all, weights_all, node_here, node_count, local_count, capacity):
    rows_all, top_count = ids_all.shape
    tok_rows = rows_all // node_count
    experts = node_count * local_count
    per_source = ids_all.reshape(node_count, tok_rows * top_count)
    onehot = (per_source[:, :, None] == jnp.arange(experts, dtype=jnp.int32)[None, None, :]).astype(
        jnp.int32
    )
    before = jnp.cumsum(onehot, axis=1) - onehot
    ranks = jnp.sum(before * onehot, axis=2)
    source = jnp.arange(node_count, dtype=jnp.int32)[:, None]
    inside = per_source // local_count == node_here
    slots = per_source % local_count * (node_count * capacity) + source * capacity + ranks
    slots = jnp.where(inside, slots, -1).reshape(rows_all, top_count)
    matches = (
        slots[None, :, :]
        == jnp.arange(local_count * node_count * capacity, dtype=jnp.int32)[:, None, None]
    )
    placing = jnp.any(matches, axis=2).astype(jnp.bfloat16)
    slot_weight = jnp.sum(jnp.where(matches, weights_all[None, :, :], 0.0), axis=(1, 2))
    return (matches, placing, slot_weight)


def per_device(tokens, cotangent, expert_ids, combine, w_gate_up, w_down):
    node_count = lax.axis_size("node")
    local_count = lax.axis_size("local")
    experts = node_count * local_count
    tok_rows, top_count = expert_ids.shape
    width = tokens.shape[1]
    capacity = max(2, 2 * tok_rows * top_count // experts)
    gate_up_one = w_gate_up[0]
    down_one = w_down[0]
    route = jnp.concatenate([expert_ids.astype(jnp.float32), combine], axis=1)
    route_all = lax.all_gather(route, "node", axis=0, tiled=True)
    ids_all = route_all[:, :top_count].astype(jnp.int32)
    weights_all = route_all[:, top_count:]
    tokens_all, cot_all = (
        lax.all_gather(tokens, "node", axis=0, tiled=True),
        lax.all_gather(cotangent, "node", axis=0, tiled=True),
    )
    matches, placing, slot_weight = node_tables(
        ids_all, weights_all, lax.axis_index("node"), node_count, local_count, capacity
    )
    send_x = jnp.dot(placing, tokens_all, preferred_element_type=jnp.float32).astype(jnp.bfloat16)
    send_x = send_x.reshape(local_count, node_count * capacity, width)
    cot_rows = jnp.dot(placing, cot_all, preferred_element_type=jnp.float32)
    send_g = (cot_rows * slot_weight[:, None]).astype(jnp.bfloat16)
    send_g = send_g.reshape(local_count, node_count * capacity, width)
    arrived, arrived_grad = (
        lax.all_to_all(send_x, "local", split_axis=0, concat_axis=0, tiled=True),
        lax.all_to_all(send_g, "local", split_axis=0, concat_axis=0, tiled=True),
    )
    output, gate, upward = expert_forward(arrived.reshape(-1, width), gate_up_one, down_one)
    back = expert_backward(arrived_grad.reshape(-1, width), gate, upward, gate_up_one, down_one)
    output = output.reshape(local_count, node_count * capacity, width)
    back = back.reshape(local_count, node_count * capacity, width)
    came_back, back_home = (
        lax.all_to_all(output, "local", split_axis=0, concat_axis=0, tiled=True),
        lax.all_to_all(back, "local", split_axis=0, concat_axis=0, tiled=True),
    )
    flat_out = came_back.reshape(-1, width).astype(jnp.float32)
    flat_back = back_home.reshape(-1, width)
    gather_rows = placing.T
    mixed_part = jnp.dot(
        gather_rows.astype(jnp.float32),
        flat_out * slot_weight[:, None],
        precision=lax.Precision.HIGHEST,
    )
    back_part = jnp.dot(gather_rows, flat_back, preferred_element_type=jnp.float32)
    slot_dot = jnp.sum(cot_rows * flat_out, axis=1)
    combine_part = jnp.sum(jnp.where(matches, slot_dot[:, None, None], 0.0), axis=0)
    mixed, grad_tokens, grad_combine = (
        lax.psum_scatter(mixed_part, "node", scatter_dimension=0, tiled=True),
        lax.psum_scatter(back_part, "node", scatter_dimension=0, tiled=True),
        lax.psum_scatter(combine_part, "node", scatter_dimension=0, tiled=True),
    )
    return (mixed.astype(jnp.bfloat16), grad_tokens.astype(jnp.bfloat16), grad_combine)


def dense_kernel(
    n,
    tok_ref,
    cot_ref,
    ids_ref,
    comb_ref,
    gate_up_hbm,
    down_hbm,
    mixed_ref,
    grad_ref,
    gcomb_ref,
    wgu,
    wd,
    xs,
    cs,
    pm,
    pb,
    gate_s,
    up_s,
    hid_s,
    cr_m,
    cr_b,
    xs_m,
    xs_b,
    xr_m,
    xr_b,
    zs_m,
    zs_b,
    zr_m,
    zr_b,
    w_sem,
    ag_send,
    ag_recv,
    core_send,
    core_recv,
    x_send,
    x_recv,
    z_send,
    z_recv,
):
    tok, width = tok_ref.shape
    top = ids_ref.shape[1]
    ff = wd.shape[0]
    z = lax.axis_index("node")
    local = lax.axis_index("local")
    x, c = local // 2, local % 2
    experts = n * 4
    me = z * 4 + local
    half = 2 * n * tok
    quarter = n * tok

    partner = {"local": (1 - x) * 2 + c}
    sibling = {"local": x * 2 + 1 - c}

    def zdev(d):
        return {"node": lax.rem(z + d, n)}

    def column(xx, cc):
        return pl.multiple_of((xx * 2 + cc) * quarter, quarter)

    def rows(xx, cc, zz):
        return pl.ds(pl.multiple_of(((xx * 2 + cc) * n + zz) * tok, tok), tok)

    load_gu = pltpu.make_async_copy(gate_up_hbm.at[0], wgu, w_sem.at[0])
    load_d = pltpu.make_async_copy(down_hbm.at[0], wd, w_sem.at[1])
    load_gu.start()
    load_d.start()

    barrier = pltpu.get_barrier_semaphore()
    for d in range(1, n):
        pl.semaphore_signal(barrier, inc=1, device_id=zdev(d), device_id_type=MESH)
    pl.semaphore_signal(barrier, inc=1, device_id=partner, device_id_type=MESH)
    pl.semaphore_signal(barrier, inc=1, device_id=sibling, device_id_type=MESH)

    mine = rows(x, c, z)
    lane = lax.broadcasted_iota(jnp.int32, (tok, LANES), 1)
    lane_expert = jnp.where(lane < experts, lane, lane - experts)
    ids = ids_ref[...]
    comb = comb_ref[...]
    weight = jnp.zeros((tok, LANES), F32)
    for k in range(top):
        weight = weight + jnp.where(ids[:, k : k + 1] == lane_expert, comb[:, k : k + 1], 0.0)
    coarse = weight.astype(BF16).astype(F32)
    xs[mine, :width] = tok_ref[...]
    xs[mine, width:] = jnp.where(lane < experts, coarse, weight - coarse).astype(BF16)
    cs[mine, :] = cot_ref[...]
    pl.semaphore_wait(barrier, n + 1)

    sends = []

    def remote(src, dst, send_sem, recv_sem, device):
        return pltpu.make_async_remote_copy(
            src_ref=src,
            dst_ref=dst,
            send_sem=send_sem,
            recv_sem=recv_sem,
            device_id=device,
            device_id_type=MESH,
        )

    def go(*args):
        copy = remote(*args)
        copy.start()
        sends.append(copy)

    bufs = (xs, cs)

    def gather_go(t, role, d, where, device):
        go(bufs[t].at[where], bufs[t].at[where], ag_send.at[t, role, d], ag_recv.at[t, role, d], device)

    def gather_wait(t, role, d, where):
        remote(
            bufs[t].at[where], bufs[t].at[where], ag_send.at[t, role, d], ag_recv.at[t, role, d], sibling
        ).wait_recv()

    def back_by(d):
        return lax.rem(z + n - d, n)

    for t in range(2):
        gather_go(t, 1, 0, mine, partner)
        for d in range(1, n):
            gather_go(t, 0, d, mine, zdev(d))
        gather_go(t, 2, 0, mine, sibling)

    def pass_z(t):
        for d in range(1, n):
            where = rows(x, c, back_by(d))
            gather_wait(t, 0, d, where)
            gather_go(t, 1, d, where, partner)
            gather_go(t, 2, d, where, sibling)

    def pass_x(t):
        for d in range(n):
            where = rows(1 - x, c, back_by(d))
            gather_wait(t, 1, d, where)
            gather_go(t, 3, d, where, sibling)

    def await_sibling(t, other):
        for d in range(n):
            where = rows(1 - x if other else x, 1 - c, back_by(d))
            gather_wait(t, 3 if other else 2, d, where)

    tile = 512 if width % 512 == 0 else width
    wide_lane = lax.broadcasted_iota(jnp.int32, (half, LANES), 1)

    def chunk(other):
        return pl.ds(pl.multiple_of((1 - x if other else x) * half, half), half)

    def my_weight(r):
        block = xs[r, width:].astype(F32)
        chosen = (wide_lane == me) | (wide_lane == me + experts)
        return jnp.sum(jnp.where(chosen, block, 0.0), axis=1, keepdims=True)

    def forward(other):
        r = chunk(other)
        projected = jnp.dot(xs[r, :width], wgu[...], preferred_element_type=F32)
        gate = projected[:, :ff]
        upward = projected[:, ff:]
        hidden = (gate * jax.nn.sigmoid(gate) * upward).astype(BF16)
        gate_s[r, :] = gate
        up_s[r, :] = upward
        hid_s[r, :] = hidden
        weight = my_weight(r)
        for j in range(width // tile):
            cols = slice(j * tile, (j + 1) * tile)
            out = jnp.dot(hidden, wd[:, cols], preferred_element_type=F32)
            pm[r, cols] = (out * weight).astype(BF16)

    across = (((1,), (1,)), ((), ()))

    def backward(other):
        r = chunk(other)
        plain = lax.dot_general(cs[r, :], wd[...], across, preferred_element_type=F32)
        gate = gate_s[r, :]
        upward = up_s[r, :]
        grads = plain * my_weight(r)
        sig = jax.nn.sigmoid(gate)
        grad_gate = grads * upward * sig * (1.0 + gate * (1.0 - sig))
        grad_up = grads * gate * sig
        dots = jnp.sum(plain * hid_s[r, :].astype(F32), axis=1, keepdims=True)
        coarse = dots.astype(BF16).astype(F32)
        pb[r, width:] = jnp.where(
            wide_lane == me, coarse, jnp.where(wide_lane == me + experts, dots - coarse, 0.0)
        ).astype(BF16)
        paired = jnp.concatenate([grad_gate, grad_up], axis=1).astype(BF16)
        for j in range(width // tile):
            cols = slice(j * tile, (j + 1) * tile)
            back = lax.dot_general(paired, wgu[cols, :], across, preferred_element_type=F32)
            pb[r, cols] = back.astype(BF16)

    parts, from_core = (pm, pb), (cr_m, cr_b)
    to_x, from_x = (xs_m, xs_b), (xr_m, xr_b)
    to_z, from_z = (zs_m, zs_b), (zr_m, zr_b)

    def core_copy(t, other):
        src = parts[t].at[pl.ds(column(1 - x if other else x, 1 - c), quarter)]
        q = 1 if other else 0
        return (src, from_core[t].at[q], core_send.at[t, q], core_recv.at[t, q], sibling)

    def core_go(t, other):
        go(*core_copy(t, other))

    def core_wait(t, other):
        remote(*core_copy(t, other)).wait_recv()

    def core_rows(d):
        return pl.ds(pl.multiple_of(lax.rem(z + d, n) * tok, tok), tok)

    def x_copy(t, d):
        return (to_x[t].at[d], from_x[t].at[d], x_send.at[t, d], x_recv.at[t, d], partner)

    def z_copy(t, d):
        return (to_z[t].at[d], from_z[t].at[d], z_send.at[t, d], z_recv.at[t, d], zdev(d))

    order = [d for d in range(1, n)] + [0]

    def send_x(t):
        core_wait(t, True)
        for d in order:
            own = parts[t][rows(1 - x, c, lax.rem(z + d, n)), :].astype(F32)
            to_x[t][d] = (own + from_core[t][1, core_rows(d), :].astype(F32)).astype(BF16)
            go(*x_copy(t, d))

    def joined(t, d):
        own = parts[t][rows(x, c, lax.rem(z + d, n)), :].astype(F32)
        return own + from_core[t][0, core_rows(d), :].astype(F32) + from_x[t][d].astype(F32)

    def send_z(t):
        core_wait(t, False)
        for d in order:
            remote(*x_copy(t, d)).wait_recv()
            if d > 0:
                to_z[t][d] = joined(t, d).astype(BF16)
                go(*z_copy(t, d))

    def finish(t):
        total = joined(t, 0)
        for d in range(1, n):
            remote(*z_copy(t, d)).wait_recv()
            total = total + from_z[t][d].astype(F32)
        return total

    pass_z(0)
    pass_z(1)
    load_gu.wait()
    load_d.wait()
    pass_x(0)
    await_sibling(0, False)
    forward(False)
    core_go(0, False)
    await_sibling(0, True)
    forward(True)
    core_go(0, True)
    await_sibling(1, False)
    backward(False)
    core_go(1, False)
    send_x(0)
    pass_x(1)
    await_sibling(1, True)
    backward(True)
    core_go(1, True)
    send_x(1)
    send_z(0)
    mixed_ref[...] = finish(0).astype(mixed_ref.dtype)
    send_z(1)
    total = finish(1)
    grad_ref[...] = total[:, :width].astype(grad_ref.dtype)
    dots = total[:, width:]
    place = lax.broadcasted_iota(jnp.int32, (tok, top), 1)
    picked = jnp.zeros((tok, top), F32)
    for k in range(top):
        value = jnp.sum(jnp.where(ids[:, k : k + 1] == lane_expert, dots, 0.0), axis=1, keepdims=True)
        picked = picked + jnp.where(place == k, value, 0.0)
    gcomb_ref[...] = picked
    for copy in sends:
        copy.wait_send()


def dense_plan(tokens, cotangent, expert_ids, combine, w_gate_up, w_down):
    n = lax.axis_size("node")
    tok, width = tokens.shape
    top = expert_ids.shape[1]
    ff = w_down.shape[1]
    total = 4 * n * tok
    wide = width + LANES
    vmem = pl.BlockSpec(memory_space=pltpu.VMEM)
    hbm = pl.BlockSpec(memory_space=pl.ANY)
    dma = pltpu.SemaphoreType.DMA
    return pl.pallas_call(
        functools.partial(dense_kernel, n),
        out_shape=(
            jax.ShapeDtypeStruct((tok, width), BF16),
            jax.ShapeDtypeStruct((tok, width), BF16),
            jax.ShapeDtypeStruct((tok, top), F32),
        ),
        in_specs=[vmem, vmem, vmem, vmem, hbm, hbm],
        out_specs=(vmem, vmem, vmem),
        scratch_shapes=[
            pltpu.VMEM((width, 2 * ff), BF16),
            pltpu.VMEM((ff, width), BF16),
            pltpu.VMEM((total, wide), BF16),
            pltpu.VMEM((total, width), BF16),
            pltpu.VMEM((total, width), BF16),
            pltpu.VMEM((total, wide), BF16),
            pltpu.VMEM((total, ff), F32),
            pltpu.VMEM((total, ff), F32),
            pltpu.VMEM((total, ff), BF16),
            pltpu.VMEM((2, n * tok, width), BF16),
            pltpu.VMEM((2, n * tok, wide), BF16),
            pltpu.VMEM((n, tok, width), BF16),
            pltpu.VMEM((n, tok, wide), BF16),
            pltpu.VMEM((n, tok, width), BF16),
            pltpu.VMEM((n, tok, wide), BF16),
            pltpu.VMEM((n, tok, width), BF16),
            pltpu.VMEM((n, tok, wide), BF16),
            pltpu.VMEM((n, tok, width), BF16),
            pltpu.VMEM((n, tok, wide), BF16),
            dma((2,)),
            dma((2, 4, n)),
            dma((2, 4, n)),
            dma((2, 2)),
            dma((2, 2)),
            dma((2, n)),
            dma((2, n)),
            dma((2, n)),
            dma((2, n)),
        ],
        compiler_params=pltpu.CompilerParams(
            collective_id=0, has_side_effects=True, vmem_limit_bytes=40 * 1024 * 1024
        ),
    )(tokens, cotangent, expert_ids, combine, w_gate_up, w_down)


def choose_plan(tokens, cotangent, expert_ids, combine, w_gate_up, w_down):
    local_count = lax.axis_size("local")
    experts = lax.axis_size("node") * local_count
    tok_rows, top_count = expert_ids.shape
    capacity = max(2, 2 * tok_rows * top_count // experts)
    dense = capacity >= tok_rows and local_count == 4 and 2 * experts <= LANES and tok_rows % 16 == 0
    plan = dense_plan if dense else per_device
    return plan(tokens, cotangent, expert_ids, combine, w_gate_up, w_down)


def solution(mesh):
    placed = (
        P(("dp", "node", "local"), None),
        P(("dp", "node", "local"), None),
        P(("dp", "node", "local"), None),
        P(("dp", "node", "local"), None),
        P(("node", "local"), None, None),
        P(("node", "local"), None, None),
    )
    return jax.shard_map(
        choose_plan,
        mesh=mesh,
        in_specs=placed,
        out_specs=(
            P(("dp", "node", "local"), None),
            P(("dp", "node", "local"), None),
            P(("dp", "node", "local"), None),
        ),
        check_vma=False,
    )
```

```python
import functools

import jax
import jax.numpy as jnp
from jax import lax
from jax.experimental import pallas as pl
from jax.experimental.pallas import tpu as pltpu
from jax.sharding import PartitionSpec as P

MESH = pl.DeviceIdType.MESH
LANES = 128
F32 = jnp.float32
BF16 = jnp.bfloat16


def expert_forward(rows, w_gate_up, w_down):
    width = w_down.shape[0]
    projected = jnp.dot(rows, w_gate_up, preferred_element_type=jnp.float32)
    gate = projected[:, :width]
    upward = projected[:, width:]
    hidden = (gate * jax.nn.sigmoid(gate) * upward).astype(jnp.bfloat16)
    output = jnp.dot(hidden, w_down, preferred_element_type=jnp.float32).astype(jnp.bfloat16)
    return (output, gate, upward)


def expert_backward(grads, gate, upward, w_gate_up, w_down):
    grad_hidden = lax.dot_general(
        grads, w_down, (((1,), (1,)), ((), ())), preferred_element_type=jnp.float32
    )
    sigmoid = jax.nn.sigmoid(gate)
    grad_gate = grad_hidden * upward * sigmoid * (1.0 + gate * (1.0 - sigmoid))
    grad_up = grad_hidden * gate * sigmoid
    paired = jnp.concatenate([grad_gate, grad_up], axis=1).astype(jnp.bfloat16)
    back = lax.dot_general(
        paired, w_gate_up, (((1,), (1,)), ((), ())), preferred_element_type=jnp.float32
    )
    return back.astype(jnp.bfloat16)


def node_tables(ids_all, weights_all, node_here, node_count, local_count, capacity):
    rows_all, top_count = ids_all.shape
    tok_rows = rows_all // node_count
    experts = node_count * local_count
    per_source = ids_all.reshape(node_count, tok_rows * top_count)
    onehot = (per_source[:, :, None] == jnp.arange(experts, dtype=jnp.int32)[None, None, :]).astype(
        jnp.int32
    )
    before = jnp.cumsum(onehot, axis=1) - onehot
    ranks = jnp.sum(before * onehot, axis=2)
    source = jnp.arange(node_count, dtype=jnp.int32)[:, None]
    inside = per_source // local_count == node_here
    slots = per_source % local_count * (node_count * capacity) + source * capacity + ranks
    slots = jnp.where(inside, slots, -1).reshape(rows_all, top_count)
    matches = (
        slots[None, :, :]
        == jnp.arange(local_count * node_count * capacity, dtype=jnp.int32)[:, None, None]
    )
    placing = jnp.any(matches, axis=2).astype(jnp.bfloat16)
    slot_weight = jnp.sum(jnp.where(matches, weights_all[None, :, :], 0.0), axis=(1, 2))
    return (matches, placing, slot_weight)


def per_device(tokens, cotangent, expert_ids, combine, w_gate_up, w_down):
    node_count = lax.axis_size("node")
    local_count = lax.axis_size("local")
    experts = node_count * local_count
    tok_rows, top_count = expert_ids.shape
    width = tokens.shape[1]
    capacity = max(2, 2 * tok_rows * top_count // experts)
    gate_up_one = w_gate_up[0]
    down_one = w_down[0]
    route = jnp.concatenate([expert_ids.astype(jnp.float32), combine], axis=1)
    route_all = lax.all_gather(route, "node", axis=0, tiled=True)
    ids_all = route_all[:, :top_count].astype(jnp.int32)
    weights_all = route_all[:, top_count:]
    tokens_all, cot_all = (
        lax.all_gather(tokens, "node", axis=0, tiled=True),
        lax.all_gather(cotangent, "node", axis=0, tiled=True),
    )
    matches, placing, slot_weight = node_tables(
        ids_all, weights_all, lax.axis_index("node"), node_count, local_count, capacity
    )
    send_x = jnp.dot(placing, tokens_all, preferred_element_type=jnp.float32).astype(jnp.bfloat16)
    send_x = send_x.reshape(local_count, node_count * capacity, width)
    cot_rows = jnp.dot(placing, cot_all, preferred_element_type=jnp.float32)
    send_g = (cot_rows * slot_weight[:, None]).astype(jnp.bfloat16)
    send_g = send_g.reshape(local_count, node_count * capacity, width)
    arrived, arrived_grad = (
        lax.all_to_all(send_x, "local", split_axis=0, concat_axis=0, tiled=True),
        lax.all_to_all(send_g, "local", split_axis=0, concat_axis=0, tiled=True),
    )
    output, gate, upward = expert_forward(arrived.reshape(-1, width), gate_up_one, down_one)
    back = expert_backward(arrived_grad.reshape(-1, width), gate, upward, gate_up_one, down_one)
    output = output.reshape(local_count, node_count * capacity, width)
    back = back.reshape(local_count, node_count * capacity, width)
    came_back, back_home = (
        lax.all_to_all(output, "local", split_axis=0, concat_axis=0, tiled=True),
        lax.all_to_all(back, "local", split_axis=0, concat_axis=0, tiled=True),
    )
    flat_out = came_back.reshape(-1, width).astype(jnp.float32)
    flat_back = back_home.reshape(-1, width)
    gather_rows = placing.T
    mixed_part = jnp.dot(
        gather_rows.astype(jnp.float32),
        flat_out * slot_weight[:, None],
        precision=lax.Precision.HIGHEST,
    )
    back_part = jnp.dot(gather_rows, flat_back, preferred_element_type=jnp.float32)
    slot_dot = jnp.sum(cot_rows * flat_out, axis=1)
    combine_part = jnp.sum(jnp.where(matches, slot_dot[:, None, None], 0.0), axis=0)
    mixed, grad_tokens, grad_combine = (
        lax.psum_scatter(mixed_part, "node", scatter_dimension=0, tiled=True),
        lax.psum_scatter(back_part, "node", scatter_dimension=0, tiled=True),
        lax.psum_scatter(combine_part, "node", scatter_dimension=0, tiled=True),
    )
    return (mixed.astype(jnp.bfloat16), grad_tokens.astype(jnp.bfloat16), grad_combine)


def dense_kernel(
    n,
    tok_hbm,
    cot_hbm,
    ids_hbm,
    comb_hbm,
    gate_up_hbm,
    down_hbm,
    mixed_ref,
    grad_ref,
    gcomb_ref,
    ids_t,
    comb_t,
    wgu,
    wd,
    xs,
    cs,
    pm,
    pb,
    gate_s,
    up_s,
    hid_s,
    cr_m,
    cr_b,
    xs_m,
    xs_b,
    xr_m,
    xr_b,
    zs_m,
    zs_b,
    zr_m,
    zr_b,
    w_sem,
    nd_send,
    ag_send,
    ag_recv,
    core_send,
    core_recv,
    x_send,
    x_recv,
    z_send,
    z_recv,
):
    tok, width = tok_hbm.shape
    top = ids_hbm.shape[0]
    ff = wd.shape[0]
    z = lax.axis_index("node")
    local = lax.axis_index("local")
    x, c = local // 2, local % 2
    experts = n * 4
    me = z * 4 + local
    half = 2 * n * tok
    quarter = n * tok

    partner = {"local": (1 - x) * 2 + c}
    sibling = {"local": x * 2 + 1 - c}

    reach = jnp.minimum(z, n - 1 - z)
    toward = jnp.where(z < n - 1 - z, 1, -1)
    near = []
    for s in range(1, n):
        turn = (s + 1) // 2 * (1 if s % 2 else -1)
        near.append(z + toward * jnp.where(s <= 2 * reach, turn, s - reach))
    far = near[::-1]

    def zdev(zz):
        return {"node": zz}

    def column(xx, cc):
        return pl.multiple_of((xx * 2 + cc) * quarter, quarter)

    def rows(xx, cc, zz):
        return pl.ds(pl.multiple_of(((xx * 2 + cc) * n + zz) * tok, tok), tok)

    mine = rows(x, c, z)
    load_own = [
        pltpu.make_async_copy(ids_hbm, ids_t, w_sem.at[2]),
        pltpu.make_async_copy(comb_hbm, comb_t, w_sem.at[3]),
        pltpu.make_async_copy(tok_hbm, xs.at[mine, pl.ds(0, width)], w_sem.at[4]),
        pltpu.make_async_copy(cot_hbm, cs.at[mine], w_sem.at[5]),
    ]
    for copy in load_own:
        copy.start()
    load_gu = pltpu.make_async_copy(gate_up_hbm.at[0], wgu, w_sem.at[0])
    load_d = pltpu.make_async_copy(down_hbm.at[0], wd, w_sem.at[1])
    load_gu.start()
    load_d.start()

    barrier = pltpu.get_barrier_semaphore()
    for zz in near:
        pl.semaphore_signal(barrier, inc=1, device_id=zdev(zz), device_id_type=MESH)
    pl.semaphore_signal(barrier, inc=1, device_id=partner, device_id_type=MESH)
    pl.semaphore_signal(barrier, inc=1, device_id=sibling, device_id_type=MESH)

    for copy in load_own:
        copy.wait()
    lane = lax.broadcasted_iota(jnp.int32, (tok, LANES), 1)
    lane_expert = jnp.where(lane < experts, lane, lane - experts)
    ids = ids_t[...].T
    comb = comb_t[...].T
    weight = jnp.zeros((tok, LANES), F32)
    for k in range(top):
        weight = weight + jnp.where(ids[:, k : k + 1] == lane_expert, comb[:, k : k + 1], 0.0)
    coarse = weight.astype(BF16).astype(F32)
    xs[mine, width:] = jnp.where(lane < experts, coarse, weight - coarse).astype(BF16)
    pl.semaphore_wait(barrier, n + 1)

    sends = []

    def remote(src, dst, send_sem, recv_sem, device):
        return pltpu.make_async_remote_copy(
            src_ref=src,
            dst_ref=dst,
            send_sem=send_sem,
            recv_sem=recv_sem,
            device_id=device,
            device_id_type=MESH,
        )

    def go(*args):
        copy = remote(*args)
        copy.start()
        sends.append(copy)

    bufs = (xs, cs)

    def gather_go(t, role, zz, where, device):
        go(bufs[t].at[where], bufs[t].at[where], ag_send.at[t, role, zz], ag_recv.at[t, role, zz], device)

    def gather_wait(t, role, zz, where):
        remote(
            bufs[t].at[where], bufs[t].at[where], ag_send.at[t, role, zz], ag_recv.at[t, role, zz], sibling
        ).wait_recv()

    for t in range(2):
        gather_go(t, 1, z, mine, partner)
        for i, zz in enumerate(near):
            go(bufs[t].at[mine], bufs[t].at[mine], nd_send.at[t, i], ag_recv.at[t, 0, z], zdev(zz))
        gather_go(t, 2, z, mine, sibling)

    def pass_z(t, places):
        for zz in places:
            where = rows(x, c, zz)
            gather_wait(t, 0, zz, where)
            gather_go(t, 1, zz, where, partner)
            gather_go(t, 2, zz, where, sibling)

    def pass_x(t):
        for zz in [z] + near:
            where = rows(1 - x, c, zz)
            gather_wait(t, 1, zz, where)
            gather_go(t, 3, zz, where, sibling)

    def await_sibling(t, other):
        for zz in [z] + near:
            where = rows(1 - x if other else x, 1 - c, zz)
            gather_wait(t, 3 if other else 2, zz, where)

    tile = 512 if width % 512 == 0 else width
    wide_lane = lax.broadcasted_iota(jnp.int32, (half, LANES), 1)

    def chunk(other):
        return pl.ds(pl.multiple_of((1 - x if other else x) * half, half), half)

    def my_weight(r):
        block = xs[r, width:].astype(F32)
        chosen = (wide_lane == me) | (wide_lane == me + experts)
        return jnp.sum(jnp.where(chosen, block, 0.0), axis=1, keepdims=True)

    def forward(other):
        r = chunk(other)
        projected = jnp.dot(xs[r, :width], wgu[...], preferred_element_type=F32)
        gate = projected[:, :ff]
        upward = projected[:, ff:]
        hidden = (gate * jax.nn.sigmoid(gate) * upward).astype(BF16)
        gate_s[r, :] = gate
        up_s[r, :] = upward
        hid_s[r, :] = hidden
        weight = my_weight(r)
        for j in range(width // tile):
            cols = slice(j * tile, (j + 1) * tile)
            out = jnp.dot(hidden, wd[:, cols], preferred_element_type=F32)
            pm[r, cols] = (out * weight).astype(BF16)

    across = (((1,), (1,)), ((), ()))

    def backward(other):
        r = chunk(other)
        plain = lax.dot_general(cs[r, :], wd[...], across, preferred_element_type=F32)
        gate = gate_s[r, :]
        upward = up_s[r, :]
        grads = plain * my_weight(r)
        sig = jax.nn.sigmoid(gate)
        grad_gate = grads * upward * sig * (1.0 + gate * (1.0 - sig))
        grad_up = grads * gate * sig
        dots = jnp.sum(plain * hid_s[r, :].astype(F32), axis=1, keepdims=True)
        coarse = dots.astype(BF16).astype(F32)
        pb[r, width:] = jnp.where(
            wide_lane == me, coarse, jnp.where(wide_lane == me + experts, dots - coarse, 0.0)
        ).astype(BF16)
        paired = jnp.concatenate([grad_gate, grad_up], axis=1).astype(BF16)
        for j in range(width // tile):
            cols = slice(j * tile, (j + 1) * tile)
            back = lax.dot_general(paired, wgu[cols, :], across, preferred_element_type=F32)
            pb[r, cols] = back.astype(BF16)

    parts, from_core = (pm, pb), (cr_m, cr_b)
    to_x, from_x = (xs_m, xs_b), (xr_m, xr_b)
    to_z, from_z = (zs_m, zs_b), (zr_m, zr_b)

    def core_copy(t, other):
        src = parts[t].at[pl.ds(column(1 - x if other else x, 1 - c), quarter)]
        q = 1 if other else 0
        return (src, from_core[t].at[q], core_send.at[t, q], core_recv.at[t, q], sibling)

    def core_go(t, other):
        go(*core_copy(t, other))

    def core_wait(t, other):
        remote(*core_copy(t, other)).wait_recv()

    def core_rows(zz):
        return pl.ds(pl.multiple_of(zz * tok, tok), tok)

    def x_copy(t, zz):
        return (to_x[t].at[zz], from_x[t].at[zz], x_send.at[t, zz], x_recv.at[t, zz], partner)

    order = far + [z]

    def send_x(t):
        core_wait(t, True)
        for zz in order:
            own = parts[t][rows(1 - x, c, zz), :].astype(F32)
            to_x[t][zz] = (own + from_core[t][1, core_rows(zz), :].astype(F32)).astype(BF16)
            go(*x_copy(t, zz))

    def joined(t, zz):
        own = parts[t][rows(x, c, zz), :].astype(F32)
        return own + from_core[t][0, core_rows(zz), :].astype(F32) + from_x[t][zz].astype(F32)

    def send_z(t):
        core_wait(t, False)
        for zz in far:
            remote(*x_copy(t, zz)).wait_recv()
            to_z[t][zz] = joined(t, zz).astype(BF16)
            go(to_z[t].at[zz], from_z[t].at[z], z_send.at[t, zz], z_recv.at[t, z], zdev(zz))

    def finish(t):
        remote(*x_copy(t, z)).wait_recv()
        total = joined(t, z)
        for zz in near:
            remote(
                to_z[t].at[zz], from_z[t].at[zz], z_send.at[t, zz], z_recv.at[t, zz], zdev(zz)
            ).wait_recv()
            total = total + from_z[t][zz].astype(F32)
        return total

    pass_z(0, near)
    load_gu.wait()
    load_d.wait()
    await_sibling(0, False)
    forward(False)
    core_go(0, False)
    pass_x(0)
    pass_z(1, near[:-1])
    await_sibling(0, True)
    forward(True)
    core_go(0, True)
    pass_z(1, near[-1:])
    send_x(0)
    await_sibling(1, False)
    backward(False)
    core_go(1, False)
    pass_x(1)
    await_sibling(1, True)
    backward(True)
    core_go(1, True)
    send_z(0)
    send_x(1)
    mixed_ref[...] = finish(0).astype(mixed_ref.dtype)
    send_z(1)
    total = finish(1)
    grad_ref[...] = total[:, :width].astype(grad_ref.dtype)
    dots = total[:, width:]
    place = lax.broadcasted_iota(jnp.int32, (tok, top), 1)
    picked = jnp.zeros((tok, top), F32)
    for k in range(top):
        value = jnp.sum(jnp.where(ids[:, k : k + 1] == lane_expert, dots, 0.0), axis=1, keepdims=True)
        picked = picked + jnp.where(place == k, value, 0.0)
    gcomb_ref[...] = picked.T
    for copy in sends:
        copy.wait_send()


def dense_plan(tokens, cotangent, expert_ids, combine, w_gate_up, w_down):
    n = lax.axis_size("node")
    tok, width = tokens.shape
    top = expert_ids.shape[1]
    ff = w_down.shape[1]
    total = 4 * n * tok
    wide = width + LANES
    vmem = pl.BlockSpec(memory_space=pltpu.VMEM)
    hbm = pl.BlockSpec(memory_space=pl.ANY)
    dma = pltpu.SemaphoreType.DMA
    mixed, grads, dots = pl.pallas_call(
        functools.partial(dense_kernel, n),
        out_shape=(
            jax.ShapeDtypeStruct((tok, width), BF16),
            jax.ShapeDtypeStruct((tok, width), BF16),
            jax.ShapeDtypeStruct((top, tok), F32),
        ),
        in_specs=[hbm] * 6,
        out_specs=(vmem, vmem, vmem),
        scratch_shapes=[
            pltpu.VMEM((top, tok), jnp.int32),
            pltpu.VMEM((top, tok), F32),
            pltpu.VMEM((width, 2 * ff), BF16),
            pltpu.VMEM((ff, width), BF16),
            pltpu.VMEM((total, wide), BF16),
            pltpu.VMEM((total, width), BF16),
            pltpu.VMEM((total, width), BF16),
            pltpu.VMEM((total, wide), BF16),
            pltpu.VMEM((total, ff), F32),
            pltpu.VMEM((total, ff), F32),
            pltpu.VMEM((total, ff), BF16),
            pltpu.VMEM((2, n * tok, width), BF16),
            pltpu.VMEM((2, n * tok, wide), BF16),
            pltpu.VMEM((n, tok, width), BF16),
            pltpu.VMEM((n, tok, wide), BF16),
            pltpu.VMEM((n, tok, width), BF16),
            pltpu.VMEM((n, tok, wide), BF16),
            pltpu.VMEM((n, tok, width), BF16),
            pltpu.VMEM((n, tok, wide), BF16),
            pltpu.VMEM((n, tok, width), BF16),
            pltpu.VMEM((n, tok, wide), BF16),
            dma((6,)),
            dma((2, n)),
            dma((2, 4, n)),
            dma((2, 4, n)),
            dma((2, 2)),
            dma((2, 2)),
            dma((2, n)),
            dma((2, n)),
            dma((2, n)),
            dma((2, n)),
        ],
        compiler_params=pltpu.CompilerParams(
            collective_id=0, has_side_effects=True, vmem_limit_bytes=62 * 1024 * 1024
        ),
    )(tokens, cotangent, expert_ids.T, combine.T, w_gate_up, w_down)
    return mixed, grads, dots.T


def choose_plan(tokens, cotangent, expert_ids, combine, w_gate_up, w_down):
    local_count = lax.axis_size("local")
    experts = lax.axis_size("node") * local_count
    tok_rows, top_count = expert_ids.shape
    capacity = max(2, 2 * tok_rows * top_count // experts)
    dense = capacity >= tok_rows and local_count == 4 and 2 * experts <= LANES and tok_rows % 16 == 0
    plan = dense_plan if dense else per_device
    return plan(tokens, cotangent, expert_ids, combine, w_gate_up, w_down)


def solution(mesh):
    placed = (
        P(("dp", "node", "local"), None),
        P(("dp", "node", "local"), None),
        P(("dp", "node", "local"), None),
        P(("dp", "node", "local"), None),
        P(("node", "local"), None, None),
        P(("node", "local"), None, None),
    )
    return jax.shard_map(
        choose_plan,
        mesh=mesh,
        in_specs=placed,
        out_specs=(
            P(("dp", "node", "local"), None),
            P(("dp", "node", "local"), None),
            P(("dp", "node", "local"), None),
        ),
        check_vma=False,
    )
```

```python
import functools

import jax
import jax.numpy as jnp
from jax import lax
from jax.experimental import pallas as pl
from jax.experimental.pallas import tpu as pltpu
from jax.sharding import PartitionSpec as P

MESH = pl.DeviceIdType.MESH
LANES = 128
F32 = jnp.float32
BF16 = jnp.bfloat16


def expert_forward(rows, w_gate_up, w_down):
    width = w_down.shape[0]
    projected = jnp.dot(rows, w_gate_up, preferred_element_type=jnp.float32)
    gate = projected[:, :width]
    upward = projected[:, width:]
    hidden = (gate * jax.nn.sigmoid(gate) * upward).astype(jnp.bfloat16)
    output = jnp.dot(hidden, w_down, preferred_element_type=jnp.float32).astype(jnp.bfloat16)
    return (output, gate, upward)


def expert_backward(grads, gate, upward, w_gate_up, w_down):
    grad_hidden = lax.dot_general(
        grads, w_down, (((1,), (1,)), ((), ())), preferred_element_type=jnp.float32
    )
    sigmoid = jax.nn.sigmoid(gate)
    grad_gate = grad_hidden * upward * sigmoid * (1.0 + gate * (1.0 - sigmoid))
    grad_up = grad_hidden * gate * sigmoid
    paired = jnp.concatenate([grad_gate, grad_up], axis=1).astype(jnp.bfloat16)
    back = lax.dot_general(
        paired, w_gate_up, (((1,), (1,)), ((), ())), preferred_element_type=jnp.float32
    )
    return back.astype(jnp.bfloat16)


def node_tables(ids_all, weights_all, node_here, node_count, local_count, capacity):
    rows_all, top_count = ids_all.shape
    tok_rows = rows_all // node_count
    experts = node_count * local_count
    per_source = ids_all.reshape(node_count, tok_rows * top_count)
    onehot = (per_source[:, :, None] == jnp.arange(experts, dtype=jnp.int32)[None, None, :]).astype(
        jnp.int32
    )
    before = jnp.cumsum(onehot, axis=1) - onehot
    ranks = jnp.sum(before * onehot, axis=2)
    source = jnp.arange(node_count, dtype=jnp.int32)[:, None]
    inside = per_source // local_count == node_here
    slots = per_source % local_count * (node_count * capacity) + source * capacity + ranks
    slots = jnp.where(inside, slots, -1).reshape(rows_all, top_count)
    matches = (
        slots[None, :, :]
        == jnp.arange(local_count * node_count * capacity, dtype=jnp.int32)[:, None, None]
    )
    placing = jnp.any(matches, axis=2).astype(jnp.bfloat16)
    slot_weight = jnp.sum(jnp.where(matches, weights_all[None, :, :], 0.0), axis=(1, 2))
    return (matches, placing, slot_weight)


def per_device(tokens, cotangent, expert_ids, combine, w_gate_up, w_down):
    node_count = lax.axis_size("node")
    local_count = lax.axis_size("local")
    experts = node_count * local_count
    tok_rows, top_count = expert_ids.shape
    width = tokens.shape[1]
    capacity = max(2, 2 * tok_rows * top_count // experts)
    gate_up_one = w_gate_up[0]
    down_one = w_down[0]
    route = jnp.concatenate([expert_ids.astype(jnp.float32), combine], axis=1)
    route_all = lax.all_gather(route, "node", axis=0, tiled=True)
    ids_all = route_all[:, :top_count].astype(jnp.int32)
    weights_all = route_all[:, top_count:]
    tokens_all, cot_all = (
        lax.all_gather(tokens, "node", axis=0, tiled=True),
        lax.all_gather(cotangent, "node", axis=0, tiled=True),
    )
    matches, placing, slot_weight = node_tables(
        ids_all, weights_all, lax.axis_index("node"), node_count, local_count, capacity
    )
    send_x = jnp.dot(placing, tokens_all, preferred_element_type=jnp.float32).astype(jnp.bfloat16)
    send_x = send_x.reshape(local_count, node_count * capacity, width)
    cot_rows = jnp.dot(placing, cot_all, preferred_element_type=jnp.float32)
    send_g = (cot_rows * slot_weight[:, None]).astype(jnp.bfloat16)
    send_g = send_g.reshape(local_count, node_count * capacity, width)
    arrived, arrived_grad = (
        lax.all_to_all(send_x, "local", split_axis=0, concat_axis=0, tiled=True),
        lax.all_to_all(send_g, "local", split_axis=0, concat_axis=0, tiled=True),
    )
    output, gate, upward = expert_forward(arrived.reshape(-1, width), gate_up_one, down_one)
    back = expert_backward(arrived_grad.reshape(-1, width), gate, upward, gate_up_one, down_one)
    output = output.reshape(local_count, node_count * capacity, width)
    back = back.reshape(local_count, node_count * capacity, width)
    came_back, back_home = (
        lax.all_to_all(output, "local", split_axis=0, concat_axis=0, tiled=True),
        lax.all_to_all(back, "local", split_axis=0, concat_axis=0, tiled=True),
    )
    flat_out = came_back.reshape(-1, width).astype(jnp.float32)
    flat_back = back_home.reshape(-1, width)
    gather_rows = placing.T
    mixed_part = jnp.dot(
        gather_rows.astype(jnp.float32),
        flat_out * slot_weight[:, None],
        precision=lax.Precision.HIGHEST,
    )
    back_part = jnp.dot(gather_rows, flat_back, preferred_element_type=jnp.float32)
    slot_dot = jnp.sum(cot_rows * flat_out, axis=1)
    combine_part = jnp.sum(jnp.where(matches, slot_dot[:, None, None], 0.0), axis=0)
    mixed, grad_tokens, grad_combine = (
        lax.psum_scatter(mixed_part, "node", scatter_dimension=0, tiled=True),
        lax.psum_scatter(back_part, "node", scatter_dimension=0, tiled=True),
        lax.psum_scatter(combine_part, "node", scatter_dimension=0, tiled=True),
    )
    return (mixed.astype(jnp.bfloat16), grad_tokens.astype(jnp.bfloat16), grad_combine)


def dense_kernel(
    n,
    tok_hbm,
    cot_hbm,
    ids_hbm,
    comb_hbm,
    gate_up_hbm,
    down_hbm,
    mixed_ref,
    grad_ref,
    gcomb_ref,
    ids_t,
    comb_t,
    wgu,
    wd,
    xs,
    cs,
    pm,
    pb,
    gate_s,
    up_s,
    hid_s,
    cr_m,
    cr_b,
    xs_m,
    xs_b,
    xr_m,
    xr_b,
    zs_m,
    zs_b,
    zr_m,
    zr_b,
    w_sem,
    nd_send,
    ag_send,
    ag_recv,
    core_send,
    core_recv,
    x_send,
    x_recv,
    z_send,
    z_recv,
):
    tok, width = tok_hbm.shape
    top = ids_hbm.shape[0]
    ff = wd.shape[0]
    z = lax.axis_index("node")
    local = lax.axis_index("local")
    x, c = local // 2, local % 2
    experts = n * 4
    me = z * 4 + local
    half = 2 * n * tok
    quarter = n * tok

    partner = {"local": (1 - x) * 2 + c}
    sibling = {"local": x * 2 + 1 - c}

    reach = jnp.minimum(z, n - 1 - z)
    toward = jnp.where(z < n - 1 - z, 1, -1)
    near = []
    for s in range(1, n):
        turn = (s + 1) // 2 * (1 if s % 2 else -1)
        near.append(z + toward * jnp.where(s <= 2 * reach, turn, s - reach))
    far = near[::-1]

    def zdev(zz):
        return {"node": zz}

    def column(xx, cc):
        return pl.multiple_of((xx * 2 + cc) * quarter, quarter)

    def rows(xx, cc, zz):
        return pl.ds(pl.multiple_of(((xx * 2 + cc) * n + zz) * tok, tok), tok)

    mine = rows(x, c, z)
    load_own = [
        pltpu.make_async_copy(ids_hbm, ids_t, w_sem.at[2]),
        pltpu.make_async_copy(comb_hbm, comb_t, w_sem.at[3]),
        pltpu.make_async_copy(tok_hbm, xs.at[mine, pl.ds(0, width)], w_sem.at[4]),
        pltpu.make_async_copy(cot_hbm, cs.at[mine], w_sem.at[5]),
    ]
    for copy in load_own:
        copy.start()
    load_gu = pltpu.make_async_copy(gate_up_hbm.at[0], wgu, w_sem.at[0])
    load_d = pltpu.make_async_copy(down_hbm.at[0], wd, w_sem.at[1])
    load_gu.start()
    load_d.start()

    barrier = pltpu.get_barrier_semaphore()
    for zz in near:
        pl.semaphore_signal(barrier, inc=1, device_id=zdev(zz), device_id_type=MESH)
    pl.semaphore_signal(barrier, inc=1, device_id=partner, device_id_type=MESH)
    pl.semaphore_signal(barrier, inc=1, device_id=sibling, device_id_type=MESH)

    for copy in load_own:
        copy.wait()
    lane = lax.broadcasted_iota(jnp.int32, (tok, LANES), 1)
    lane_expert = jnp.where(lane < experts, lane, lane - experts)
    ids = ids_t[...].T
    comb = comb_t[...].T
    weight = jnp.zeros((tok, LANES), F32)
    for k in range(top):
        weight = weight + jnp.where(ids[:, k : k + 1] == lane_expert, comb[:, k : k + 1], 0.0)
    coarse = weight.astype(BF16).astype(F32)
    xs[mine, width:] = jnp.where(lane < experts, coarse, weight - coarse).astype(BF16)
    pl.semaphore_wait(barrier, n + 1)

    sends = []
    maybe = []

    def remote(src, dst, send_sem, recv_sem, device):
        return pltpu.make_async_remote_copy(
            src_ref=src,
            dst_ref=dst,
            send_sem=send_sem,
            recv_sem=recv_sem,
            device_id=device,
            device_id_type=MESH,
        )

    def go(*args):
        copy = remote(*args)
        copy.start()
        sends.append(copy)

    bufs = (xs, cs)

    def gather_go(t, role, zz, where, device):
        go(bufs[t].at[where], bufs[t].at[where], ag_send.at[t, role, zz], ag_recv.at[t, role, zz], device)

    def gather_wait(t, role, zz, where):
        remote(
            bufs[t].at[where], bufs[t].at[where], ag_send.at[t, role, zz], ag_recv.at[t, role, zz], sibling
        ).wait_recv()

    def inside(zz):
        return (zz >= 0) & (zz < n)

    def go_if(cond, *args):
        copy = remote(*args)
        pl.when(cond)(copy.start)
        maybe.append((cond, copy))

    def own_go(t):
        for i, to in enumerate((z - 1, z + 1)):
            device = zdev(jnp.clip(to, 0, n - 1))
            block = bufs[t].at[mine]
            go_if(inside(to), block, block, nd_send.at[t, i], ag_recv.at[t, 0, z], device)
        gather_go(t, 1, z, mine, partner)
        gather_go(t, 2, z, mine, sibling)

    def pass_z(t, s):
        for side in (-1, 1):
            here = inside(z + side * s)
            zz = jnp.clip(z + side * s, 0, n - 1)
            to = z - side
            where = rows(x, c, zz)
            block = bufs[t].at[where]
            pl.when(here)(functools.partial(gather_wait, t, 0, zz, where))
            if s < n - 1:
                device = zdev(jnp.clip(to, 0, n - 1))
                go_if(here & inside(to), block, block, ag_send.at[t, 0, zz], ag_recv.at[t, 0, zz], device)
            go_if(here, block, block, ag_send.at[t, 1, zz], ag_recv.at[t, 1, zz], partner)
            go_if(here, block, block, ag_send.at[t, 2, zz], ag_recv.at[t, 2, zz], sibling)

    def pass_x(t):
        for zz in [z] + near:
            where = rows(1 - x, c, zz)
            gather_wait(t, 1, zz, where)
            gather_go(t, 3, zz, where, sibling)

    def await_sibling(t, other):
        for zz in [z] + near:
            where = rows(1 - x if other else x, 1 - c, zz)
            gather_wait(t, 3 if other else 2, zz, where)

    tile = 512 if width % 512 == 0 else width
    wide_lane = lax.broadcasted_iota(jnp.int32, (half, LANES), 1)

    def chunk(other):
        return pl.ds(pl.multiple_of((1 - x if other else x) * half, half), half)

    def my_weight(r):
        block = xs[r, width:].astype(F32)
        chosen = (wide_lane == me) | (wide_lane == me + experts)
        return jnp.sum(jnp.where(chosen, block, 0.0), axis=1, keepdims=True)

    def forward(other):
        r = chunk(other)
        projected = jnp.dot(xs[r, :width], wgu[...], preferred_element_type=F32)
        gate = projected[:, :ff]
        upward = projected[:, ff:]
        hidden = (gate * jax.nn.sigmoid(gate) * upward).astype(BF16)
        gate_s[r, :] = gate
        up_s[r, :] = upward
        hid_s[r, :] = hidden
        weight = my_weight(r)
        for j in range(width // tile):
            cols = slice(j * tile, (j + 1) * tile)
            out = jnp.dot(hidden, wd[:, cols], preferred_element_type=F32)
            pm[r, cols] = (out * weight).astype(BF16)

    across = (((1,), (1,)), ((), ()))

    def backward(other):
        r = chunk(other)
        plain = lax.dot_general(cs[r, :], wd[...], across, preferred_element_type=F32)
        gate = gate_s[r, :]
        upward = up_s[r, :]
        grads = plain * my_weight(r)
        sig = jax.nn.sigmoid(gate)
        grad_gate = grads * upward * sig * (1.0 + gate * (1.0 - sig))
        grad_up = grads * gate * sig
        dots = jnp.sum(plain * hid_s[r, :].astype(F32), axis=1, keepdims=True)
        coarse = dots.astype(BF16).astype(F32)
        pb[r, width:] = jnp.where(
            wide_lane == me, coarse, jnp.where(wide_lane == me + experts, dots - coarse, 0.0)
        ).astype(BF16)
        paired = jnp.concatenate([grad_gate, grad_up], axis=1).astype(BF16)
        for j in range(width // tile):
            cols = slice(j * tile, (j + 1) * tile)
            back = lax.dot_general(paired, wgu[cols, :], across, preferred_element_type=F32)
            pb[r, cols] = back.astype(BF16)

    parts, from_core = (pm, pb), (cr_m, cr_b)
    to_x, from_x = (xs_m, xs_b), (xr_m, xr_b)
    to_z, from_z = (zs_m, zs_b), (zr_m, zr_b)

    def core_copy(t, other):
        src = parts[t].at[pl.ds(column(1 - x if other else x, 1 - c), quarter)]
        q = 1 if other else 0
        return (src, from_core[t].at[q], core_send.at[t, q], core_recv.at[t, q], sibling)

    def core_go(t, other):
        go(*core_copy(t, other))

    def core_wait(t, other):
        remote(*core_copy(t, other)).wait_recv()

    def core_rows(zz):
        return pl.ds(pl.multiple_of(zz * tok, tok), tok)

    def x_copy(t, zz):
        return (to_x[t].at[zz], from_x[t].at[zz], x_send.at[t, zz], x_recv.at[t, zz], partner)

    order = far + [z]

    def send_x(t):
        core_wait(t, True)
        for zz in order:
            own = parts[t][rows(1 - x, c, zz), :].astype(F32)
            to_x[t][zz] = (own + from_core[t][1, core_rows(zz), :].astype(F32)).astype(BF16)
            go(*x_copy(t, zz))

    def joined(t, zz):
        own = parts[t][rows(x, c, zz), :].astype(F32)
        return own + from_core[t][0, core_rows(zz), :].astype(F32) + from_x[t][zz].astype(F32)

    def send_z(t):
        core_wait(t, False)
        for zz in far:
            remote(*x_copy(t, zz)).wait_recv()
            to_z[t][zz] = joined(t, zz).astype(BF16)
            go(to_z[t].at[zz], from_z[t].at[z], z_send.at[t, zz], z_recv.at[t, z], zdev(zz))

    def finish(t):
        remote(*x_copy(t, z)).wait_recv()
        total = joined(t, z)
        for zz in near:
            remote(
                to_z[t].at[zz], from_z[t].at[zz], z_send.at[t, zz], z_recv.at[t, zz], zdev(zz)
            ).wait_recv()
            total = total + from_z[t][zz].astype(F32)
        return total

    own_go(0)
    for s in range(1, n):
        pass_z(0, s)
        if s == 1:
            own_go(1)
        if s == 2:
            pass_z(1, 1)
    load_gu.wait()
    load_d.wait()
    await_sibling(0, False)
    forward(False)
    core_go(0, False)
    for s in range(min(2, n - 1), n):
        pass_z(1, s)
    pass_x(0)
    await_sibling(0, True)
    forward(True)
    core_go(0, True)
    send_x(0)
    await_sibling(1, False)
    backward(False)
    core_go(1, False)
    pass_x(1)
    await_sibling(1, True)
    backward(True)
    core_go(1, True)
    send_z(0)
    send_x(1)
    mixed_ref[...] = finish(0).astype(mixed_ref.dtype)
    send_z(1)
    total = finish(1)
    grad_ref[...] = total[:, :width].astype(grad_ref.dtype)
    dots = total[:, width:]
    place = lax.broadcasted_iota(jnp.int32, (tok, top), 1)
    picked = jnp.zeros((tok, top), F32)
    for k in range(top):
        value = jnp.sum(jnp.where(ids[:, k : k + 1] == lane_expert, dots, 0.0), axis=1, keepdims=True)
        picked = picked + jnp.where(place == k, value, 0.0)
    gcomb_ref[...] = picked.T
    for copy in sends:
        copy.wait_send()
    for cond, copy in maybe:
        pl.when(cond)(copy.wait_send)


def dense_plan(tokens, cotangent, expert_ids, combine, w_gate_up, w_down):
    n = lax.axis_size("node")
    tok, width = tokens.shape
    top = expert_ids.shape[1]
    ff = w_down.shape[1]
    total = 4 * n * tok
    wide = width + LANES
    vmem = pl.BlockSpec(memory_space=pltpu.VMEM)
    hbm = pl.BlockSpec(memory_space=pl.ANY)
    dma = pltpu.SemaphoreType.DMA
    mixed, grads, dots = pl.pallas_call(
        functools.partial(dense_kernel, n),
        out_shape=(
            jax.ShapeDtypeStruct((tok, width), BF16),
            jax.ShapeDtypeStruct((tok, width), BF16),
            jax.ShapeDtypeStruct((top, tok), F32),
        ),
        in_specs=[hbm] * 6,
        out_specs=(vmem, vmem, vmem),
        scratch_shapes=[
            pltpu.VMEM((top, tok), jnp.int32),
            pltpu.VMEM((top, tok), F32),
            pltpu.VMEM((width, 2 * ff), BF16),
            pltpu.VMEM((ff, width), BF16),
            pltpu.VMEM((total, wide), BF16),
            pltpu.VMEM((total, width), BF16),
            pltpu.VMEM((total, width), BF16),
            pltpu.VMEM((total, wide), BF16),
            pltpu.VMEM((total, ff), F32),
            pltpu.VMEM((total, ff), F32),
            pltpu.VMEM((total, ff), BF16),
            pltpu.VMEM((2, n * tok, width), BF16),
            pltpu.VMEM((2, n * tok, wide), BF16),
            pltpu.VMEM((n, tok, width), BF16),
            pltpu.VMEM((n, tok, wide), BF16),
            pltpu.VMEM((n, tok, width), BF16),
            pltpu.VMEM((n, tok, wide), BF16),
            pltpu.VMEM((n, tok, width), BF16),
            pltpu.VMEM((n, tok, wide), BF16),
            pltpu.VMEM((n, tok, width), BF16),
            pltpu.VMEM((n, tok, wide), BF16),
            dma((6,)),
            dma((2, n)),
            dma((2, 4, n)),
            dma((2, 4, n)),
            dma((2, 2)),
            dma((2, 2)),
            dma((2, n)),
            dma((2, n)),
            dma((2, n)),
            dma((2, n)),
        ],
        compiler_params=pltpu.CompilerParams(
            collective_id=0, has_side_effects=True, vmem_limit_bytes=62 * 1024 * 1024
        ),
    )(tokens, cotangent, expert_ids.T, combine.T, w_gate_up, w_down)
    return mixed, grads, dots.T


def choose_plan(tokens, cotangent, expert_ids, combine, w_gate_up, w_down):
    local_count = lax.axis_size("local")
    experts = lax.axis_size("node") * local_count
    tok_rows, top_count = expert_ids.shape
    capacity = max(2, 2 * tok_rows * top_count // experts)
    dense = capacity >= tok_rows and local_count == 4 and 2 * experts <= LANES and tok_rows % 16 == 0
    plan = dense_plan if dense else per_device
    return plan(tokens, cotangent, expert_ids, combine, w_gate_up, w_down)


def solution(mesh):
    placed = (
        P(("dp", "node", "local"), None),
        P(("dp", "node", "local"), None),
        P(("dp", "node", "local"), None),
        P(("dp", "node", "local"), None),
        P(("node", "local"), None, None),
        P(("node", "local"), None, None),
    )
    return jax.shard_map(
        choose_plan,
        mesh=mesh,
        in_specs=placed,
        out_specs=(
            P(("dp", "node", "local"), None),
            P(("dp", "node", "local"), None),
            P(("dp", "node", "local"), None),
        ),
        check_vma=False,
    )
```

```python
import functools

import jax
import jax.numpy as jnp
from jax import lax
from jax.experimental import pallas as pl
from jax.experimental.pallas import tpu as pltpu
from jax.sharding import PartitionSpec as P

MESH = pl.DeviceIdType.MESH
LANES = 128
F32 = jnp.float32
BF16 = jnp.bfloat16


def expert_forward(rows, w_gate_up, w_down):
    width = w_down.shape[0]
    projected = jnp.dot(rows, w_gate_up, preferred_element_type=jnp.float32)
    gate = projected[:, :width]
    upward = projected[:, width:]
    hidden = (gate * jax.nn.sigmoid(gate) * upward).astype(jnp.bfloat16)
    output = jnp.dot(hidden, w_down, preferred_element_type=jnp.float32).astype(jnp.bfloat16)
    return (output, gate, upward)


def expert_backward(grads, gate, upward, w_gate_up, w_down):
    grad_hidden = lax.dot_general(
        grads, w_down, (((1,), (1,)), ((), ())), preferred_element_type=jnp.float32
    )
    sigmoid = jax.nn.sigmoid(gate)
    grad_gate = grad_hidden * upward * sigmoid * (1.0 + gate * (1.0 - sigmoid))
    grad_up = grad_hidden * gate * sigmoid
    paired = jnp.concatenate([grad_gate, grad_up], axis=1).astype(jnp.bfloat16)
    back = lax.dot_general(
        paired, w_gate_up, (((1,), (1,)), ((), ())), preferred_element_type=jnp.float32
    )
    return back.astype(jnp.bfloat16)


def node_tables(ids_all, weights_all, node_here, node_count, local_count, capacity):
    rows_all, top_count = ids_all.shape
    tok_rows = rows_all // node_count
    experts = node_count * local_count
    per_source = ids_all.reshape(node_count, tok_rows * top_count)
    onehot = (per_source[:, :, None] == jnp.arange(experts, dtype=jnp.int32)[None, None, :]).astype(
        jnp.int32
    )
    before = jnp.cumsum(onehot, axis=1) - onehot
    ranks = jnp.sum(before * onehot, axis=2)
    source = jnp.arange(node_count, dtype=jnp.int32)[:, None]
    inside = per_source // local_count == node_here
    slots = per_source % local_count * (node_count * capacity) + source * capacity + ranks
    slots = jnp.where(inside, slots, -1).reshape(rows_all, top_count)
    matches = (
        slots[None, :, :]
        == jnp.arange(local_count * node_count * capacity, dtype=jnp.int32)[:, None, None]
    )
    placing = jnp.any(matches, axis=2).astype(jnp.bfloat16)
    slot_weight = jnp.sum(jnp.where(matches, weights_all[None, :, :], 0.0), axis=(1, 2))
    return (matches, placing, slot_weight)


def per_device(tokens, cotangent, expert_ids, combine, w_gate_up, w_down):
    node_count = lax.axis_size("node")
    local_count = lax.axis_size("local")
    experts = node_count * local_count
    tok_rows, top_count = expert_ids.shape
    width = tokens.shape[1]
    capacity = max(2, 2 * tok_rows * top_count // experts)
    gate_up_one = w_gate_up[0]
    down_one = w_down[0]
    route = jnp.concatenate([expert_ids.astype(jnp.float32), combine], axis=1)
    route_all = lax.all_gather(route, "node", axis=0, tiled=True)
    ids_all = route_all[:, :top_count].astype(jnp.int32)
    weights_all = route_all[:, top_count:]
    tokens_all, cot_all = (
        lax.all_gather(tokens, "node", axis=0, tiled=True),
        lax.all_gather(cotangent, "node", axis=0, tiled=True),
    )
    matches, placing, slot_weight = node_tables(
        ids_all, weights_all, lax.axis_index("node"), node_count, local_count, capacity
    )
    send_x = jnp.dot(placing, tokens_all, preferred_element_type=jnp.float32).astype(jnp.bfloat16)
    send_x = send_x.reshape(local_count, node_count * capacity, width)
    cot_rows = jnp.dot(placing, cot_all, preferred_element_type=jnp.float32)
    send_g = (cot_rows * slot_weight[:, None]).astype(jnp.bfloat16)
    send_g = send_g.reshape(local_count, node_count * capacity, width)
    arrived, arrived_grad = (
        lax.all_to_all(send_x, "local", split_axis=0, concat_axis=0, tiled=True),
        lax.all_to_all(send_g, "local", split_axis=0, concat_axis=0, tiled=True),
    )
    output, gate, upward = expert_forward(arrived.reshape(-1, width), gate_up_one, down_one)
    back = expert_backward(arrived_grad.reshape(-1, width), gate, upward, gate_up_one, down_one)
    output = output.reshape(local_count, node_count * capacity, width)
    back = back.reshape(local_count, node_count * capacity, width)
    came_back, back_home = (
        lax.all_to_all(output, "local", split_axis=0, concat_axis=0, tiled=True),
        lax.all_to_all(back, "local", split_axis=0, concat_axis=0, tiled=True),
    )
    flat_out = came_back.reshape(-1, width).astype(jnp.float32)
    flat_back = back_home.reshape(-1, width)
    gather_rows = placing.T
    mixed_part = jnp.dot(
        gather_rows.astype(jnp.float32),
        flat_out * slot_weight[:, None],
        precision=lax.Precision.HIGHEST,
    )
    back_part = jnp.dot(gather_rows, flat_back, preferred_element_type=jnp.float32)
    slot_dot = jnp.sum(cot_rows * flat_out, axis=1)
    combine_part = jnp.sum(jnp.where(matches, slot_dot[:, None, None], 0.0), axis=0)
    mixed, grad_tokens, grad_combine = (
        lax.psum_scatter(mixed_part, "node", scatter_dimension=0, tiled=True),
        lax.psum_scatter(back_part, "node", scatter_dimension=0, tiled=True),
        lax.psum_scatter(combine_part, "node", scatter_dimension=0, tiled=True),
    )
    return (mixed.astype(jnp.bfloat16), grad_tokens.astype(jnp.bfloat16), grad_combine)


def dense_kernel(
    n,
    tok_hbm,
    cot_hbm,
    ids_hbm,
    comb_hbm,
    gate_up_hbm,
    down_hbm,
    mixed_ref,
    grad_ref,
    gcomb_ref,
    ids_t,
    comb_t,
    wgu,
    wd,
    xs,
    cs,
    pm,
    pb,
    gate_s,
    up_s,
    hid_s,
    pair_s,
    cr_m,
    cr_b,
    xs_m,
    xs_b,
    xr_m,
    xr_b,
    zs_m,
    zs_b,
    zr_m,
    zr_b,
    w_sem,
    nd_send,
    ag_send,
    ag_recv,
    core_send,
    core_recv,
    x_send,
    x_recv,
    z_send,
    z_recv,
):
    tok, width = tok_hbm.shape
    top = ids_hbm.shape[0]
    ff = wd.shape[0]
    z = lax.axis_index("node")
    local = lax.axis_index("local")
    x, c = local // 2, local % 2
    experts = n * 4
    me = z * 4 + local
    half = 2 * n * tok
    quarter = n * tok

    partner = {"local": (1 - x) * 2 + c}
    sibling = {"local": x * 2 + 1 - c}

    reach = jnp.minimum(z, n - 1 - z)
    toward = jnp.where(z < n - 1 - z, 1, -1)
    near = []
    for s in range(1, n):
        turn = (s + 1) // 2 * (1 if s % 2 else -1)
        near.append(z + toward * jnp.where(s <= 2 * reach, turn, s - reach))
    far = near[::-1]

    def zdev(zz):
        return {"node": zz}

    def column(xx, cc):
        return pl.multiple_of((xx * 2 + cc) * quarter, quarter)

    def rows(xx, cc, zz):
        return pl.ds(pl.multiple_of(((xx * 2 + cc) * n + zz) * tok, tok), tok)

    mine = rows(x, c, z)
    load_own = [
        pltpu.make_async_copy(ids_hbm, ids_t, w_sem.at[2]),
        pltpu.make_async_copy(comb_hbm, comb_t, w_sem.at[3]),
        pltpu.make_async_copy(tok_hbm, xs.at[mine, pl.ds(0, width)], w_sem.at[4]),
        pltpu.make_async_copy(cot_hbm, cs.at[mine], w_sem.at[5]),
    ]
    for copy in load_own:
        copy.start()
    load_gu = pltpu.make_async_copy(gate_up_hbm.at[0], wgu, w_sem.at[0])
    load_d = pltpu.make_async_copy(down_hbm.at[0], wd, w_sem.at[1])
    load_gu.start()
    load_d.start()

    barrier = pltpu.get_barrier_semaphore()
    for zz in near:
        pl.semaphore_signal(barrier, inc=1, device_id=zdev(zz), device_id_type=MESH)
    pl.semaphore_signal(barrier, inc=1, device_id=partner, device_id_type=MESH)
    pl.semaphore_signal(barrier, inc=1, device_id=sibling, device_id_type=MESH)

    for copy in load_own:
        copy.wait()
    lane = lax.broadcasted_iota(jnp.int32, (tok, LANES), 1)
    lane_expert = jnp.where(lane < experts, lane, lane - experts)
    ids = ids_t[...].T
    comb = comb_t[...].T
    weight = jnp.zeros((tok, LANES), F32)
    for k in range(top):
        weight = weight + jnp.where(ids[:, k : k + 1] == lane_expert, comb[:, k : k + 1], 0.0)
    coarse = weight.astype(BF16).astype(F32)
    xs[mine, width:] = jnp.where(lane < experts, coarse, weight - coarse).astype(BF16)
    pl.semaphore_wait(barrier, n + 1)

    sends = []
    maybe = []

    def remote(src, dst, send_sem, recv_sem, device):
        return pltpu.make_async_remote_copy(
            src_ref=src,
            dst_ref=dst,
            send_sem=send_sem,
            recv_sem=recv_sem,
            device_id=device,
            device_id_type=MESH,
        )

    def go(*args):
        copy = remote(*args)
        copy.start()
        sends.append(copy)

    bufs = (xs, cs)

    def gather_go(t, role, zz, where, device):
        go(bufs[t].at[where], bufs[t].at[where], ag_send.at[t, role, zz], ag_recv.at[t, role, zz], device)

    def gather_wait(t, role, zz, where):
        remote(
            bufs[t].at[where], bufs[t].at[where], ag_send.at[t, role, zz], ag_recv.at[t, role, zz], sibling
        ).wait_recv()

    def inside(zz):
        return (zz >= 0) & (zz < n)

    def go_if(cond, *args):
        copy = remote(*args)
        pl.when(cond)(copy.start)
        maybe.append((cond, copy))

    def own_go(t):
        for i, to in enumerate((z - 1, z + 1)):
            device = zdev(jnp.clip(to, 0, n - 1))
            block = bufs[t].at[mine]
            go_if(inside(to), block, block, nd_send.at[t, i], ag_recv.at[t, 0, z], device)
        gather_go(t, 1, z, mine, partner)
        gather_go(t, 2, z, mine, sibling)

    def pass_z(t, s):
        for side in (-1, 1):
            here = inside(z + side * s)
            zz = jnp.clip(z + side * s, 0, n - 1)
            to = z - side
            where = rows(x, c, zz)
            block = bufs[t].at[where]
            pl.when(here)(functools.partial(gather_wait, t, 0, zz, where))
            if s < n - 1:
                device = zdev(jnp.clip(to, 0, n - 1))
                go_if(here & inside(to), block, block, ag_send.at[t, 0, zz], ag_recv.at[t, 0, zz], device)
            go_if(here, block, block, ag_send.at[t, 1, zz], ag_recv.at[t, 1, zz], partner)
            go_if(here, block, block, ag_send.at[t, 2, zz], ag_recv.at[t, 2, zz], sibling)

    def pass_x(t):
        for zz in [z] + near:
            where = rows(1 - x, c, zz)
            gather_wait(t, 1, zz, where)
            gather_go(t, 3, zz, where, sibling)

    def await_sibling(t, other):
        for zz in [z] + near:
            where = rows(1 - x if other else x, 1 - c, zz)
            gather_wait(t, 3 if other else 2, zz, where)

    tile = 512 if width % 512 == 0 else width
    total_rows = 2 * half
    wide_lane = lax.broadcasted_iota(jnp.int32, (total_rows, LANES), 1)

    def my_weight():
        block = xs[:, width:].astype(F32)
        chosen = (wide_lane == me) | (wide_lane == me + experts)
        return jnp.sum(jnp.where(chosen, block, 0.0), axis=1, keepdims=True)

    def forward():
        projected = jnp.dot(xs[:, :width], wgu[...], preferred_element_type=F32)
        gate = projected[:, :ff]
        upward = projected[:, ff:]
        hidden = (gate * jax.nn.sigmoid(gate) * upward).astype(BF16)
        gate_s[...] = gate
        up_s[...] = upward
        hid_s[...] = hidden
        weight = my_weight()

        @pl.loop(0, width // tile)
        def _(j):
            cols = pl.ds(pl.multiple_of(j * tile, tile), tile)
            out = jnp.dot(hid_s[...], wd[:, cols], preferred_element_type=F32)
            pm[:, cols] = (out * weight).astype(BF16)

    across = (((1,), (1,)), ((), ()))

    def backward():
        plain = lax.dot_general(cs[...], wd[...], across, preferred_element_type=F32)
        gate = gate_s[...]
        upward = up_s[...]
        grads = plain * my_weight()
        sig = jax.nn.sigmoid(gate)
        grad_gate = grads * upward * sig * (1.0 + gate * (1.0 - sig))
        grad_up = grads * gate * sig
        dots = jnp.sum(plain * hid_s[...].astype(F32), axis=1, keepdims=True)
        coarse = dots.astype(BF16).astype(F32)
        pb[:, width:] = jnp.where(
            wide_lane == me, coarse, jnp.where(wide_lane == me + experts, dots - coarse, 0.0)
        ).astype(BF16)
        pair_s[:, :ff] = grad_gate.astype(BF16)
        pair_s[:, ff:] = grad_up.astype(BF16)

        @pl.loop(0, width // tile)
        def _(j):
            cols = pl.ds(pl.multiple_of(j * tile, tile), tile)
            back = lax.dot_general(pair_s[...], wgu[cols, :], across, preferred_element_type=F32)
            pb[:, cols] = back.astype(BF16)

    parts, from_core = (pm, pb), (cr_m, cr_b)
    to_x, from_x = (xs_m, xs_b), (xr_m, xr_b)
    to_z, from_z = (zs_m, zs_b), (zr_m, zr_b)

    def core_copy(t, other):
        src = parts[t].at[pl.ds(column(1 - x if other else x, 1 - c), quarter)]
        q = 1 if other else 0
        return (src, from_core[t].at[q], core_send.at[t, q], core_recv.at[t, q], sibling)

    def core_go(t, other):
        go(*core_copy(t, other))

    def core_wait(t, other):
        remote(*core_copy(t, other)).wait_recv()

    def core_rows(zz):
        return pl.ds(pl.multiple_of(zz * tok, tok), tok)

    def x_copy(t, zz):
        return (to_x[t].at[zz], from_x[t].at[zz], x_send.at[t, zz], x_recv.at[t, zz], partner)

    order = far + [z]

    def send_x(t):
        core_wait(t, True)
        for zz in order:
            own = parts[t][rows(1 - x, c, zz), :].astype(F32)
            to_x[t][zz] = (own + from_core[t][1, core_rows(zz), :].astype(F32)).astype(BF16)
            go(*x_copy(t, zz))

    def joined(t, zz):
        own = parts[t][rows(x, c, zz), :].astype(F32)
        return own + from_core[t][0, core_rows(zz), :].astype(F32) + from_x[t][zz].astype(F32)

    def send_z(t):
        core_wait(t, False)
        for zz in far:
            remote(*x_copy(t, zz)).wait_recv()
            to_z[t][zz] = joined(t, zz).astype(BF16)
            go(to_z[t].at[zz], from_z[t].at[z], z_send.at[t, zz], z_recv.at[t, z], zdev(zz))

    def finish(t):
        remote(*x_copy(t, z)).wait_recv()
        total = joined(t, z)
        for zz in near:
            remote(
                to_z[t].at[zz], from_z[t].at[zz], z_send.at[t, zz], z_recv.at[t, zz], zdev(zz)
            ).wait_recv()
            total = total + from_z[t][zz].astype(F32)
        return total

    own_go(0)
    for s in range(1, n):
        pass_z(0, s)
        if s == 1:
            own_go(1)
        if s == 2:
            pass_z(1, 1)
    pass_x(0)
    for s in range(min(2, n - 1), n):
        pass_z(1, s)
    load_gu.wait()
    load_d.wait()
    await_sibling(0, False)
    await_sibling(0, True)
    forward()
    core_go(0, True)
    core_go(0, False)
    pass_x(1)
    send_x(0)
    await_sibling(1, False)
    await_sibling(1, True)
    backward()
    core_go(1, True)
    core_go(1, False)
    send_z(0)
    send_x(1)
    mixed_ref[...] = finish(0).astype(mixed_ref.dtype)
    send_z(1)
    total = finish(1)
    grad_ref[...] = total[:, :width].astype(grad_ref.dtype)
    dots = total[:, width:]
    place = lax.broadcasted_iota(jnp.int32, (tok, top), 1)
    picked = jnp.zeros((tok, top), F32)
    for k in range(top):
        value = jnp.sum(jnp.where(ids[:, k : k + 1] == lane_expert, dots, 0.0), axis=1, keepdims=True)
        picked = picked + jnp.where(place == k, value, 0.0)
    gcomb_ref[...] = picked.T
    for copy in sends:
        copy.wait_send()
    for cond, copy in maybe:
        pl.when(cond)(copy.wait_send)


def dense_plan(tokens, cotangent, expert_ids, combine, w_gate_up, w_down):
    n = lax.axis_size("node")
    tok, width = tokens.shape
    top = expert_ids.shape[1]
    ff = w_down.shape[1]
    total = 4 * n * tok
    wide = width + LANES
    vmem = pl.BlockSpec(memory_space=pltpu.VMEM)
    hbm = pl.BlockSpec(memory_space=pl.ANY)
    dma = pltpu.SemaphoreType.DMA
    mixed, grads, dots = pl.pallas_call(
        functools.partial(dense_kernel, n),
        out_shape=(
            jax.ShapeDtypeStruct((tok, width), BF16),
            jax.ShapeDtypeStruct((tok, width), BF16),
            jax.ShapeDtypeStruct((top, tok), F32),
        ),
        in_specs=[hbm] * 6,
        out_specs=(vmem, vmem, vmem),
        scratch_shapes=[
            pltpu.VMEM((top, tok), jnp.int32),
            pltpu.VMEM((top, tok), F32),
            pltpu.VMEM((width, 2 * ff), BF16),
            pltpu.VMEM((ff, width), BF16),
            pltpu.VMEM((total, wide), BF16),
            pltpu.VMEM((total, width), BF16),
            pltpu.VMEM((total, width), BF16),
            pltpu.VMEM((total, wide), BF16),
            pltpu.VMEM((total, ff), F32),
            pltpu.VMEM((total, ff), F32),
            pltpu.VMEM((total, ff), BF16),
            pltpu.VMEM((total, 2 * ff), BF16),
            pltpu.VMEM((2, n * tok, width), BF16),
            pltpu.VMEM((2, n * tok, wide), BF16),
            pltpu.VMEM((n, tok, width), BF16),
            pltpu.VMEM((n, tok, wide), BF16),
            pltpu.VMEM((n, tok, width), BF16),
            pltpu.VMEM((n, tok, wide), BF16),
            pltpu.VMEM((n, tok, width), BF16),
            pltpu.VMEM((n, tok, wide), BF16),
            pltpu.VMEM((n, tok, width), BF16),
            pltpu.VMEM((n, tok, wide), BF16),
            dma((6,)),
            dma((2, n)),
            dma((2, 4, n)),
            dma((2, 4, n)),
            dma((2, 2)),
            dma((2, 2)),
            dma((2, n)),
            dma((2, n)),
            dma((2, n)),
            dma((2, n)),
        ],
        compiler_params=pltpu.CompilerParams(
            collective_id=0, has_side_effects=True, vmem_limit_bytes=62 * 1024 * 1024
        ),
    )(tokens, cotangent, expert_ids.T, combine.T, w_gate_up, w_down)
    return mixed, grads, dots.T


def choose_plan(tokens, cotangent, expert_ids, combine, w_gate_up, w_down):
    local_count = lax.axis_size("local")
    experts = lax.axis_size("node") * local_count
    tok_rows, top_count = expert_ids.shape
    capacity = max(2, 2 * tok_rows * top_count // experts)
    dense = capacity >= tok_rows and local_count == 4 and 2 * experts <= LANES and tok_rows % 16 == 0
    plan = dense_plan if dense else per_device
    return plan(tokens, cotangent, expert_ids, combine, w_gate_up, w_down)


def solution(mesh):
    placed = (
        P(("dp", "node", "local"), None),
        P(("dp", "node", "local"), None),
        P(("dp", "node", "local"), None),
        P(("dp", "node", "local"), None),
        P(("node", "local"), None, None),
        P(("node", "local"), None, None),
    )
    return jax.shard_map(
        choose_plan,
        mesh=mesh,
        in_specs=placed,
        out_specs=(
            P(("dp", "node", "local"), None),
            P(("dp", "node", "local"), None),
            P(("dp", "node", "local"), None),
        ),
        check_vma=False,
    )
```

```python
import functools

import jax
import jax.numpy as jnp
from jax import lax
from jax.experimental import pallas as pl
from jax.experimental.pallas import tpu as pltpu
from jax.sharding import PartitionSpec as P

MESH = pl.DeviceIdType.MESH
LANES = 128
F32 = jnp.float32
BF16 = jnp.bfloat16


def expert_forward(rows, w_gate_up, w_down):
    width = w_down.shape[0]
    projected = jnp.dot(rows, w_gate_up, preferred_element_type=jnp.float32)
    gate = projected[:, :width]
    upward = projected[:, width:]
    hidden = (gate * jax.nn.sigmoid(gate) * upward).astype(jnp.bfloat16)
    output = jnp.dot(hidden, w_down, preferred_element_type=jnp.float32).astype(jnp.bfloat16)
    return (output, gate, upward)


def expert_backward(grads, gate, upward, w_gate_up, w_down):
    grad_hidden = lax.dot_general(
        grads, w_down, (((1,), (1,)), ((), ())), preferred_element_type=jnp.float32
    )
    sigmoid = jax.nn.sigmoid(gate)
    grad_gate = grad_hidden * upward * sigmoid * (1.0 + gate * (1.0 - sigmoid))
    grad_up = grad_hidden * gate * sigmoid
    paired = jnp.concatenate([grad_gate, grad_up], axis=1).astype(jnp.bfloat16)
    back = lax.dot_general(
        paired, w_gate_up, (((1,), (1,)), ((), ())), preferred_element_type=jnp.float32
    )
    return back.astype(jnp.bfloat16)


def node_tables(ids_all, weights_all, node_here, node_count, local_count, capacity):
    rows_all, top_count = ids_all.shape
    tok_rows = rows_all // node_count
    experts = node_count * local_count
    per_source = ids_all.reshape(node_count, tok_rows * top_count)
    onehot = (per_source[:, :, None] == jnp.arange(experts, dtype=jnp.int32)[None, None, :]).astype(
        jnp.int32
    )
    before = jnp.cumsum(onehot, axis=1) - onehot
    ranks = jnp.sum(before * onehot, axis=2)
    source = jnp.arange(node_count, dtype=jnp.int32)[:, None]
    inside = per_source // local_count == node_here
    slots = per_source % local_count * (node_count * capacity) + source * capacity + ranks
    slots = jnp.where(inside, slots, -1).reshape(rows_all, top_count)
    matches = (
        slots[None, :, :]
        == jnp.arange(local_count * node_count * capacity, dtype=jnp.int32)[:, None, None]
    )
    placing = jnp.any(matches, axis=2).astype(jnp.bfloat16)
    slot_weight = jnp.sum(jnp.where(matches, weights_all[None, :, :], 0.0), axis=(1, 2))
    return (matches, placing, slot_weight)


def per_device(tokens, cotangent, expert_ids, combine, w_gate_up, w_down):
    node_count = lax.axis_size("node")
    local_count = lax.axis_size("local")
    experts = node_count * local_count
    tok_rows, top_count = expert_ids.shape
    width = tokens.shape[1]
    capacity = max(2, 2 * tok_rows * top_count // experts)
    gate_up_one = w_gate_up[0]
    down_one = w_down[0]
    route = jnp.concatenate([expert_ids.astype(jnp.float32), combine], axis=1)
    route_all = lax.all_gather(route, "node", axis=0, tiled=True)
    ids_all = route_all[:, :top_count].astype(jnp.int32)
    weights_all = route_all[:, top_count:]
    tokens_all, cot_all = (
        lax.all_gather(tokens, "node", axis=0, tiled=True),
        lax.all_gather(cotangent, "node", axis=0, tiled=True),
    )
    matches, placing, slot_weight = node_tables(
        ids_all, weights_all, lax.axis_index("node"), node_count, local_count, capacity
    )
    send_x = jnp.dot(placing, tokens_all, preferred_element_type=jnp.float32).astype(jnp.bfloat16)
    send_x = send_x.reshape(local_count, node_count * capacity, width)
    cot_rows = jnp.dot(placing, cot_all, preferred_element_type=jnp.float32)
    send_g = (cot_rows * slot_weight[:, None]).astype(jnp.bfloat16)
    send_g = send_g.reshape(local_count, node_count * capacity, width)
    arrived, arrived_grad = (
        lax.all_to_all(send_x, "local", split_axis=0, concat_axis=0, tiled=True),
        lax.all_to_all(send_g, "local", split_axis=0, concat_axis=0, tiled=True),
    )
    output, gate, upward = expert_forward(arrived.reshape(-1, width), gate_up_one, down_one)
    back = expert_backward(arrived_grad.reshape(-1, width), gate, upward, gate_up_one, down_one)
    output = output.reshape(local_count, node_count * capacity, width)
    back = back.reshape(local_count, node_count * capacity, width)
    came_back, back_home = (
        lax.all_to_all(output, "local", split_axis=0, concat_axis=0, tiled=True),
        lax.all_to_all(back, "local", split_axis=0, concat_axis=0, tiled=True),
    )
    flat_out = came_back.reshape(-1, width).astype(jnp.float32)
    flat_back = back_home.reshape(-1, width)
    gather_rows = placing.T
    mixed_part = jnp.dot(
        gather_rows.astype(jnp.float32),
        flat_out * slot_weight[:, None],
        precision=lax.Precision.HIGHEST,
    )
    back_part = jnp.dot(gather_rows, flat_back, preferred_element_type=jnp.float32)
    slot_dot = jnp.sum(cot_rows * flat_out, axis=1)
    combine_part = jnp.sum(jnp.where(matches, slot_dot[:, None, None], 0.0), axis=0)
    mixed, grad_tokens, grad_combine = (
        lax.psum_scatter(mixed_part, "node", scatter_dimension=0, tiled=True),
        lax.psum_scatter(back_part, "node", scatter_dimension=0, tiled=True),
        lax.psum_scatter(combine_part, "node", scatter_dimension=0, tiled=True),
    )
    return (mixed.astype(jnp.bfloat16), grad_tokens.astype(jnp.bfloat16), grad_combine)


def dense_kernel(
    n,
    tiles,
    tok_hbm,
    cot_hbm,
    ids_hbm,
    comb_hbm,
    gate_up_hbm,
    down_hbm,
    mixed_ref,
    grad_ref,
    gcomb_ref,
    ids_t,
    comb_t,
    wgu,
    wd,
    xs,
    cs,
    gate_s,
    up_s,
    hid_s,
    pair_s,
    parts,
    from_core,
    to_x,
    from_x,
    to_z,
    from_z,
    w_sem,
    nd_send,
    ag_send,
    ag_recv,
    core_send,
    core_recv,
    x_send,
    x_recv,
    z_send,
    z_recv,
):
    tok, width = tok_hbm.shape
    top = ids_hbm.shape[0]
    ff = wd.shape[0]
    z = lax.axis_index("node")
    local = lax.axis_index("local")
    x, c = local // 2, local % 2
    experts = n * 4
    me = z * 4 + local
    half = 2 * n * tok
    quarter = n * tok
    tile = width // tiles

    partner = {"local": (1 - x) * 2 + c}
    sibling = {"local": x * 2 + 1 - c}

    reach = jnp.minimum(z, n - 1 - z)
    toward = jnp.where(z < n - 1 - z, 1, -1)
    near = []
    for s in range(1, n):
        turn = (s + 1) // 2 * (1 if s % 2 else -1)
        near.append(z + toward * jnp.where(s <= 2 * reach, turn, s - reach))
    far = near[::-1]

    def zdev(zz):
        return {"node": zz}

    def column(xx, cc):
        return pl.multiple_of((xx * 2 + cc) * quarter, quarter)

    def rows(xx, cc, zz):
        return pl.ds(pl.multiple_of(((xx * 2 + cc) * n + zz) * tok, tok), tok)

    mine = rows(x, c, z)
    load_own = [
        pltpu.make_async_copy(ids_hbm, ids_t, w_sem.at[2]),
        pltpu.make_async_copy(comb_hbm, comb_t, w_sem.at[3]),
        pltpu.make_async_copy(tok_hbm, xs.at[mine, pl.ds(0, width)], w_sem.at[4]),
        pltpu.make_async_copy(cot_hbm, cs.at[mine], w_sem.at[5]),
    ]
    for copy in load_own:
        copy.start()
    load_gu = pltpu.make_async_copy(gate_up_hbm.at[0], wgu, w_sem.at[0])
    load_d = pltpu.make_async_copy(down_hbm.at[0], wd, w_sem.at[1])
    load_gu.start()
    load_d.start()

    barrier = pltpu.get_barrier_semaphore()
    for zz in near:
        pl.semaphore_signal(barrier, inc=1, device_id=zdev(zz), device_id_type=MESH)
    pl.semaphore_signal(barrier, inc=1, device_id=partner, device_id_type=MESH)
    pl.semaphore_signal(barrier, inc=1, device_id=sibling, device_id_type=MESH)

    for copy in load_own:
        copy.wait()
    lane = lax.broadcasted_iota(jnp.int32, (tok, LANES), 1)
    lane_expert = jnp.where(lane < experts, lane, lane - experts)
    ids = ids_t[...].T
    comb = comb_t[...].T
    weight = jnp.zeros((tok, LANES), F32)
    for k in range(top):
        weight = weight + jnp.where(ids[:, k : k + 1] == lane_expert, comb[:, k : k + 1], 0.0)
    coarse = weight.astype(BF16).astype(F32)
    xs[mine, width:] = jnp.where(lane < experts, coarse, weight - coarse).astype(BF16)
    pl.semaphore_wait(barrier, n + 1)

    sends = []
    maybe = []

    def remote(src, dst, send_sem, recv_sem, device):
        return pltpu.make_async_remote_copy(
            src_ref=src,
            dst_ref=dst,
            send_sem=send_sem,
            recv_sem=recv_sem,
            device_id=device,
            device_id_type=MESH,
        )

    def go(*args):
        copy = remote(*args)
        copy.start()
        sends.append(copy)

    bufs = (xs, cs)

    def gather_go(t, role, zz, where, device):
        go(bufs[t].at[where], bufs[t].at[where], ag_send.at[t, role, zz], ag_recv.at[t, role, zz], device)

    def gather_wait(t, role, zz, where):
        remote(
            bufs[t].at[where], bufs[t].at[where], ag_send.at[t, role, zz], ag_recv.at[t, role, zz], sibling
        ).wait_recv()

    def inside(zz):
        return (zz >= 0) & (zz < n)

    def go_if(cond, *args):
        copy = remote(*args)
        pl.when(cond)(copy.start)
        maybe.append((cond, copy))

    def own_go_z(t):
        for i, to in enumerate((z - 1, z + 1)):
            device = zdev(jnp.clip(to, 0, n - 1))
            block = bufs[t].at[mine]
            go_if(inside(to), block, block, nd_send.at[t, i], ag_recv.at[t, 0, z], device)

    def own_go_near(t):
        gather_go(t, 1, z, mine, partner)
        gather_go(t, 2, z, mine, sibling)

    def own_go(t):
        own_go_near(t)
        own_go_z(t)

    def pass_z(t, s):
        for side in (-1, 1):
            here = inside(z + side * s)
            zz = jnp.clip(z + side * s, 0, n - 1)
            to = z - side
            where = rows(x, c, zz)
            block = bufs[t].at[where]
            pl.when(here)(functools.partial(gather_wait, t, 0, zz, where))
            if s < n - 1:
                device = zdev(jnp.clip(to, 0, n - 1))
                go_if(here & inside(to), block, block, ag_send.at[t, 0, zz], ag_recv.at[t, 0, zz], device)
            go_if(here, block, block, ag_send.at[t, 1, zz], ag_recv.at[t, 1, zz], partner)
            go_if(here, block, block, ag_send.at[t, 2, zz], ag_recv.at[t, 2, zz], sibling)

    def pass_x(t):
        for zz in [z] + near:
            where = rows(1 - x, c, zz)
            gather_wait(t, 1, zz, where)
            gather_go(t, 3, zz, where, sibling)

    def await_sibling(t, other):
        for zz in [z] + near:
            where = rows(1 - x if other else x, 1 - c, zz)
            gather_wait(t, 3 if other else 2, zz, where)

    total_rows = 2 * half
    wide_lane = lax.broadcasted_iota(jnp.int32, (total_rows, LANES), 1)

    def my_weight():
        block = xs[:, width:].astype(F32)
        chosen = (wide_lane == me) | (wide_lane == me + experts)
        return jnp.sum(jnp.where(chosen, block, 0.0), axis=1, keepdims=True)

    def forward_hidden():
        projected = jnp.dot(xs[:, :width], wgu[...], preferred_element_type=F32)
        gate = projected[:, :ff]
        upward = projected[:, ff:]
        gate_s[...] = gate
        up_s[...] = upward
        hid_s[...] = (gate * jax.nn.sigmoid(gate) * upward).astype(BF16)

    def forward_tile(j, weight):
        cols = slice(j * tile, (j + 1) * tile)
        out = jnp.dot(hid_s[...], wd[:, cols], preferred_element_type=F32)
        parts[j][...] = (out * weight).astype(BF16)

    across = (((1,), (1,)), ((), ()))

    def backward_hidden(weight):
        plain = lax.dot_general(cs[...], wd[...], across, preferred_element_type=F32)
        gate = gate_s[...]
        upward = up_s[...]
        grads = plain * weight
        sig = jax.nn.sigmoid(gate)
        grad_gate = grads * upward * sig * (1.0 + gate * (1.0 - sig))
        grad_up = grads * gate * sig
        dots = jnp.sum(plain * hid_s[...].astype(F32), axis=1, keepdims=True)
        coarse = dots.astype(BF16).astype(F32)
        parts[tiles][...] = jnp.where(
            wide_lane == me, coarse, jnp.where(wide_lane == me + experts, dots - coarse, 0.0)
        ).astype(BF16)
        pair_s[:, :ff] = grad_gate.astype(BF16)
        pair_s[:, ff:] = grad_up.astype(BF16)

    def backward_tile(j):
        cols = slice(j * tile, (j + 1) * tile)
        back = lax.dot_general(pair_s[...], wgu[cols, :], across, preferred_element_type=F32)
        parts[tiles + 1 + j][...] = back.astype(BF16)

    def core_copy(i, other):
        src = parts[i].at[pl.ds(column(1 - x if other else x, 1 - c), quarter)]
        q = 1 if other else 0
        return (src, from_core[i].at[q], core_send.at[i, q], core_recv.at[i, q], sibling)

    def core_go(i):
        go(*core_copy(i, True))
        go(*core_copy(i, False))

    def x_copy(i):
        return (to_x[i], from_x[i], x_send.at[i], x_recv.at[i], partner)

    def x_stage(i):
        remote(*core_copy(i, True)).wait_recv()
        own = parts[i][pl.ds(column(1 - x, c), quarter), :].astype(F32)
        to_x[i][...] = (own + from_core[i][1].astype(F32)).astype(BF16)
        go(*x_copy(i))

    def place(zz):
        return pl.ds(pl.multiple_of(zz * tok, tok), tok)

    def z_stage(i):
        remote(*core_copy(i, False)).wait_recv()
        remote(*x_copy(i)).wait_recv()
        own = parts[i][pl.ds(column(x, c), quarter), :].astype(F32)
        to_z[i][...] = (own + from_core[i][0].astype(F32) + from_x[i][...].astype(F32)).astype(BF16)
        for zz in far:
            go(to_z[i].at[place(zz)], from_z[i].at[place(z)], z_send.at[i, zz], z_recv.at[i, z], zdev(zz))

    def finish(i):
        total = parts[i][mine, :].astype(F32)
        total = total + from_core[i][0, place(z), :].astype(F32) + from_x[i][place(z), :].astype(F32)
        for zz in near:
            block = from_z[i].at[place(zz)]
            remote(to_z[i].at[place(zz)], block, z_send.at[i, zz], z_recv.at[i, zz], zdev(zz)).wait_recv()
            total = total + block[...].astype(F32)
        return total

    own_go(0)
    pass_z(0, 1)
    own_go_z(1)
    for s in range(2, n):
        pass_z(0, s)
    own_go_near(1)
    pass_z(1, 1)
    pass_x(0)
    if n > 2:
        pass_z(1, 2)
    load_gu.wait()
    load_d.wait()
    await_sibling(0, False)
    await_sibling(0, True)
    forward_hidden()
    for s in range(3, n):
        pass_z(1, s)
    weight = my_weight()
    for j in range(tiles):
        forward_tile(j, weight)
        core_go(j)
        if j > 0:
            x_stage(j - 1)
    pass_x(1)
    x_stage(tiles - 1)
    await_sibling(1, False)
    await_sibling(1, True)
    backward_hidden(weight)
    core_go(tiles)
    for j in range(tiles):
        backward_tile(j)
        core_go(tiles + 1 + j)
        x_stage(tiles + j)
        z_stage(j)
    x_stage(2 * tiles)
    for i in range(tiles, 2 * tiles + 1):
        z_stage(i)
    for j in range(tiles):
        mixed_ref[:, j * tile : (j + 1) * tile] = finish(j).astype(mixed_ref.dtype)
    dots = finish(tiles)
    for j in range(tiles):
        grad_ref[:, j * tile : (j + 1) * tile] = finish(tiles + 1 + j).astype(grad_ref.dtype)
    choice = lax.broadcasted_iota(jnp.int32, (tok, top), 1)
    picked = jnp.zeros((tok, top), F32)
    for k in range(top):
        value = jnp.sum(jnp.where(ids[:, k : k + 1] == lane_expert, dots, 0.0), axis=1, keepdims=True)
        picked = picked + jnp.where(choice == k, value, 0.0)
    gcomb_ref[...] = picked.T
    for copy in sends:
        copy.wait_send()
    for cond, copy in maybe:
        pl.when(cond)(copy.wait_send)


def dense_plan(tokens, cotangent, expert_ids, combine, w_gate_up, w_down):
    n = lax.axis_size("node")
    tok, width = tokens.shape
    top = expert_ids.shape[1]
    ff = w_down.shape[1]
    total = 4 * n * tok
    wide = width + LANES
    vmem = pl.BlockSpec(memory_space=pltpu.VMEM)
    hbm = pl.BlockSpec(memory_space=pl.ANY)
    dma = pltpu.SemaphoreType.DMA
    tiles = 4 if width % 1024 == 0 else 1
    count = 2 * tiles + 1

    def pieces(*lead):
        sums = [pltpu.VMEM((*lead, width // tiles), BF16)] * tiles
        return [*sums, pltpu.VMEM((*lead, LANES), BF16), *sums]

    mixed, grads, dots = pl.pallas_call(
        functools.partial(dense_kernel, n, tiles),
        out_shape=(
            jax.ShapeDtypeStruct((tok, width), BF16),
            jax.ShapeDtypeStruct((tok, width), BF16),
            jax.ShapeDtypeStruct((top, tok), F32),
        ),
        in_specs=[hbm] * 6,
        out_specs=(vmem, vmem, vmem),
        scratch_shapes=[
            pltpu.VMEM((top, tok), jnp.int32),
            pltpu.VMEM((top, tok), F32),
            pltpu.VMEM((width, 2 * ff), BF16),
            pltpu.VMEM((ff, width), BF16),
            pltpu.VMEM((total, wide), BF16),
            pltpu.VMEM((total, width), BF16),
            pltpu.VMEM((total, ff), F32),
            pltpu.VMEM((total, ff), F32),
            pltpu.VMEM((total, ff), BF16),
            pltpu.VMEM((total, 2 * ff), BF16),
            pieces(total),
            pieces(2, n * tok),
            pieces(n * tok),
            pieces(n * tok),
            pieces(n * tok),
            pieces(n * tok),
            dma((6,)),
            dma((2, n)),
            dma((2, 4, n)),
            dma((2, 4, n)),
            dma((count, 2)),
            dma((count, 2)),
            dma((count,)),
            dma((count,)),
            dma((count, n)),
            dma((count, n)),
        ],
        compiler_params=pltpu.CompilerParams(
            collective_id=0, has_side_effects=True, vmem_limit_bytes=62 * 1024 * 1024
        ),
    )(tokens, cotangent, expert_ids.T, combine.T, w_gate_up, w_down)
    return mixed, grads, dots.T


def choose_plan(tokens, cotangent, expert_ids, combine, w_gate_up, w_down):
    local_count = lax.axis_size("local")
    experts = lax.axis_size("node") * local_count
    tok_rows, top_count = expert_ids.shape
    capacity = max(2, 2 * tok_rows * top_count // experts)
    dense = capacity >= tok_rows and local_count == 4 and 2 * experts <= LANES and tok_rows % 16 == 0
    plan = dense_plan if dense else per_device
    return plan(tokens, cotangent, expert_ids, combine, w_gate_up, w_down)


def solution(mesh):
    placed = (
        P(("dp", "node", "local"), None),
        P(("dp", "node", "local"), None),
        P(("dp", "node", "local"), None),
        P(("dp", "node", "local"), None),
        P(("node", "local"), None, None),
        P(("node", "local"), None, None),
    )
    return jax.shard_map(
        choose_plan,
        mesh=mesh,
        in_specs=placed,
        out_specs=(
            P(("dp", "node", "local"), None),
            P(("dp", "node", "local"), None),
            P(("dp", "node", "local"), None),
        ),
        check_vma=False,
    )
```

```python
import functools

import jax
import jax.numpy as jnp
from jax import lax
from jax.experimental import pallas as pl
from jax.experimental.pallas import tpu as pltpu
from jax.sharding import PartitionSpec as P

MESH = pl.DeviceIdType.MESH
LANES = 128
F32 = jnp.float32
BF16 = jnp.bfloat16


def expert_forward(rows, w_gate_up, w_down):
    width = w_down.shape[0]
    projected = jnp.dot(rows, w_gate_up, preferred_element_type=jnp.float32)
    gate = projected[:, :width]
    upward = projected[:, width:]
    hidden = (gate * jax.nn.sigmoid(gate) * upward).astype(jnp.bfloat16)
    output = jnp.dot(hidden, w_down, preferred_element_type=jnp.float32).astype(jnp.bfloat16)
    return (output, gate, upward)


def expert_backward(grads, gate, upward, w_gate_up, w_down):
    grad_hidden = lax.dot_general(
        grads, w_down, (((1,), (1,)), ((), ())), preferred_element_type=jnp.float32
    )
    sigmoid = jax.nn.sigmoid(gate)
    grad_gate = grad_hidden * upward * sigmoid * (1.0 + gate * (1.0 - sigmoid))
    grad_up = grad_hidden * gate * sigmoid
    paired = jnp.concatenate([grad_gate, grad_up], axis=1).astype(jnp.bfloat16)
    back = lax.dot_general(
        paired, w_gate_up, (((1,), (1,)), ((), ())), preferred_element_type=jnp.float32
    )
    return back.astype(jnp.bfloat16)


def node_tables(ids_all, weights_all, node_here, node_count, local_count, capacity):
    rows_all, top_count = ids_all.shape
    tok_rows = rows_all // node_count
    experts = node_count * local_count
    per_source = ids_all.reshape(node_count, tok_rows * top_count)
    onehot = (per_source[:, :, None] == jnp.arange(experts, dtype=jnp.int32)[None, None, :]).astype(
        jnp.int32
    )
    before = jnp.cumsum(onehot, axis=1) - onehot
    ranks = jnp.sum(before * onehot, axis=2)
    source = jnp.arange(node_count, dtype=jnp.int32)[:, None]
    inside = per_source // local_count == node_here
    slots = per_source % local_count * (node_count * capacity) + source * capacity + ranks
    slots = jnp.where(inside, slots, -1).reshape(rows_all, top_count)
    matches = (
        slots[None, :, :]
        == jnp.arange(local_count * node_count * capacity, dtype=jnp.int32)[:, None, None]
    )
    placing = jnp.any(matches, axis=2).astype(jnp.bfloat16)
    slot_weight = jnp.sum(jnp.where(matches, weights_all[None, :, :], 0.0), axis=(1, 2))
    return (matches, placing, slot_weight)


def per_device(tokens, cotangent, expert_ids, combine, w_gate_up, w_down):
    node_count = lax.axis_size("node")
    local_count = lax.axis_size("local")
    experts = node_count * local_count
    tok_rows, top_count = expert_ids.shape
    width = tokens.shape[1]
    capacity = max(2, 2 * tok_rows * top_count // experts)
    gate_up_one = w_gate_up[0]
    down_one = w_down[0]
    route = jnp.concatenate([expert_ids.astype(jnp.float32), combine], axis=1)
    route_all = lax.all_gather(route, "node", axis=0, tiled=True)
    ids_all = route_all[:, :top_count].astype(jnp.int32)
    weights_all = route_all[:, top_count:]
    tokens_all, cot_all = (
        lax.all_gather(tokens, "node", axis=0, tiled=True),
        lax.all_gather(cotangent, "node", axis=0, tiled=True),
    )
    matches, placing, slot_weight = node_tables(
        ids_all, weights_all, lax.axis_index("node"), node_count, local_count, capacity
    )
    send_x = jnp.dot(placing, tokens_all, preferred_element_type=jnp.float32).astype(jnp.bfloat16)
    send_x = send_x.reshape(local_count, node_count * capacity, width)
    cot_rows = jnp.dot(placing, cot_all, preferred_element_type=jnp.float32)
    send_g = (cot_rows * slot_weight[:, None]).astype(jnp.bfloat16)
    send_g = send_g.reshape(local_count, node_count * capacity, width)
    arrived, arrived_grad = (
        lax.all_to_all(send_x, "local", split_axis=0, concat_axis=0, tiled=True),
        lax.all_to_all(send_g, "local", split_axis=0, concat_axis=0, tiled=True),
    )
    output, gate, upward = expert_forward(arrived.reshape(-1, width), gate_up_one, down_one)
    back = expert_backward(arrived_grad.reshape(-1, width), gate, upward, gate_up_one, down_one)
    output = output.reshape(local_count, node_count * capacity, width)
    back = back.reshape(local_count, node_count * capacity, width)
    came_back, back_home = (
        lax.all_to_all(output, "local", split_axis=0, concat_axis=0, tiled=True),
        lax.all_to_all(back, "local", split_axis=0, concat_axis=0, tiled=True),
    )
    flat_out = came_back.reshape(-1, width).astype(jnp.float32)
    flat_back = back_home.reshape(-1, width)
    gather_rows = placing.T
    mixed_part = jnp.dot(
        gather_rows.astype(jnp.float32),
        flat_out * slot_weight[:, None],
        precision=lax.Precision.HIGHEST,
    )
    back_part = jnp.dot(gather_rows, flat_back, preferred_element_type=jnp.float32)
    slot_dot = jnp.sum(cot_rows * flat_out, axis=1)
    combine_part = jnp.sum(jnp.where(matches, slot_dot[:, None, None], 0.0), axis=0)
    mixed, grad_tokens, grad_combine = (
        lax.psum_scatter(mixed_part, "node", scatter_dimension=0, tiled=True),
        lax.psum_scatter(back_part, "node", scatter_dimension=0, tiled=True),
        lax.psum_scatter(combine_part, "node", scatter_dimension=0, tiled=True),
    )
    return (mixed.astype(jnp.bfloat16), grad_tokens.astype(jnp.bfloat16), grad_combine)


def dense_kernel(
    n,
    tok_hbm,
    cot_hbm,
    ids_hbm,
    comb_hbm,
    gate_up_hbm,
    down_hbm,
    mixed_ref,
    grad_ref,
    gcomb_ref,
    ids_t,
    comb_t,
    wgu,
    wd,
    xs,
    cs,
    pm,
    pb,
    gate_s,
    up_s,
    hid_s,
    pair_s,
    cr_m,
    cr_b,
    xs_m,
    xs_b,
    xr_m,
    xr_b,
    zs_m,
    zs_b,
    zr_m,
    zr_b,
    w_sem,
    nd_send,
    ag_send,
    ag_recv,
    core_send,
    core_recv,
    x_send,
    x_recv,
    z_send,
    z_recv,
):
    tok, width = tok_hbm.shape
    top = ids_hbm.shape[0]
    ff = wd.shape[0]
    z = lax.axis_index("node")
    local = lax.axis_index("local")
    x, c = local // 2, local % 2
    experts = n * 4
    me = z * 4 + local
    half = 2 * n * tok
    quarter = n * tok

    partner = {"local": (1 - x) * 2 + c}
    sibling = {"local": x * 2 + 1 - c}

    reach = jnp.minimum(z, n - 1 - z)
    toward = jnp.where(z < n - 1 - z, 1, -1)
    near = []
    for s in range(1, n):
        turn = (s + 1) // 2 * (1 if s % 2 else -1)
        near.append(z + toward * jnp.where(s <= 2 * reach, turn, s - reach))
    far = near[::-1]

    def zdev(zz):
        return {"node": zz}

    def column(xx, cc):
        return pl.multiple_of((xx * 2 + cc) * quarter, quarter)

    def rows(xx, cc, zz):
        return pl.ds(pl.multiple_of(((xx * 2 + cc) * n + zz) * tok, tok), tok)

    mine = rows(x, c, z)
    load_own = [
        pltpu.make_async_copy(ids_hbm, ids_t, w_sem.at[2]),
        pltpu.make_async_copy(comb_hbm, comb_t, w_sem.at[3]),
        pltpu.make_async_copy(tok_hbm, xs.at[mine, pl.ds(0, width)], w_sem.at[4]),
        pltpu.make_async_copy(cot_hbm, cs.at[mine], w_sem.at[5]),
    ]
    for copy in load_own:
        copy.start()
    load_gu = pltpu.make_async_copy(gate_up_hbm.at[0], wgu, w_sem.at[0])
    load_d = pltpu.make_async_copy(down_hbm.at[0], wd, w_sem.at[1])
    load_gu.start()
    load_d.start()

    barrier = pltpu.get_barrier_semaphore()
    for zz in near:
        pl.semaphore_signal(barrier, inc=1, device_id=zdev(zz), device_id_type=MESH)
    pl.semaphore_signal(barrier, inc=1, device_id=partner, device_id_type=MESH)
    pl.semaphore_signal(barrier, inc=1, device_id=sibling, device_id_type=MESH)

    for copy in load_own:
        copy.wait()
    lane = lax.broadcasted_iota(jnp.int32, (tok, LANES), 1)
    lane_expert = jnp.where(lane < experts, lane, lane - experts)
    ids = ids_t[...].T
    comb = comb_t[...].T
    weight = jnp.zeros((tok, LANES), F32)
    for k in range(top):
        weight = weight + jnp.where(ids[:, k : k + 1] == lane_expert, comb[:, k : k + 1], 0.0)
    coarse = weight.astype(BF16).astype(F32)
    xs[mine, width:] = jnp.where(lane < experts, coarse, weight - coarse).astype(BF16)
    pl.semaphore_wait(barrier, n + 1)

    sends = []
    maybe = []

    def remote(src, dst, send_sem, recv_sem, device):
        return pltpu.make_async_remote_copy(
            src_ref=src,
            dst_ref=dst,
            send_sem=send_sem,
            recv_sem=recv_sem,
            device_id=device,
            device_id_type=MESH,
        )

    def go(*args):
        copy = remote(*args)
        copy.start()
        sends.append(copy)

    bufs = (xs, cs)

    def gather_go(t, role, zz, where, device):
        go(bufs[t].at[where], bufs[t].at[where], ag_send.at[t, role, zz], ag_recv.at[t, role, zz], device)

    def gather_wait(t, role, zz, where):
        remote(
            bufs[t].at[where], bufs[t].at[where], ag_send.at[t, role, zz], ag_recv.at[t, role, zz], sibling
        ).wait_recv()

    def inside(zz):
        return (zz >= 0) & (zz < n)

    def go_if(cond, *args):
        copy = remote(*args)
        pl.when(cond)(copy.start)
        maybe.append((cond, copy))

    def own_go(t):
        for i, to in enumerate((z - 1, z + 1)):
            device = zdev(jnp.clip(to, 0, n - 1))
            block = bufs[t].at[mine]
            go_if(inside(to), block, block, nd_send.at[t, i], ag_recv.at[t, 0, z], device)
        gather_go(t, 1, z, mine, partner)
        gather_go(t, 2, z, mine, sibling)

    paired = n % 2 == 0 and n >= 4
    mate = z + 1 - 2 * lax.rem(z, 2)
    at_end = (z == 0) | (z == n - 1)

    def over_x(t, zz):
        if not paired:
            return zz >= 0
        return (zz != mate) | at_end if t == 0 else zz != mate

    def pass_z(t, s):
        for side in (-1, 1):
            here = inside(z + side * s)
            zz = jnp.clip(z + side * s, 0, n - 1)
            to = z - side
            where = rows(x, c, zz)
            block = bufs[t].at[where]
            pl.when(here)(functools.partial(gather_wait, t, 0, zz, where))
            if s < n - 1:
                device = zdev(jnp.clip(to, 0, n - 1))
                go_if(here & inside(to), block, block, ag_send.at[t, 0, zz], ag_recv.at[t, 0, zz], device)
            go_if(here & over_x(t, zz), block, block, ag_send.at[t, 1, zz], ag_recv.at[t, 1, zz], partner)
            go_if(here, block, block, ag_send.at[t, 2, zz], ag_recv.at[t, 2, zz], sibling)

    def pass_x(t):
        for zz in [z] + near:
            where = rows(1 - x, c, zz)
            gather_wait(t, 1, zz, where)
            if paired and zz is z:
                block = bufs[t].at[where]
                give = (mate > 0) & (mate < n - 1) if t == 0 else z >= 0
                go_if(give, block, block, nd_send.at[t, 2], ag_recv.at[t, 1, z], zdev(mate))
            gather_go(t, 3, zz, where, sibling)

    def await_sibling(t, other):
        for zz in [z] + near:
            where = rows(1 - x if other else x, 1 - c, zz)
            gather_wait(t, 3 if other else 2, zz, where)

    tile = 512 if width % 512 == 0 else width
    total_rows = 2 * half
    wide_lane = lax.broadcasted_iota(jnp.int32, (total_rows, LANES), 1)

    def my_weight():
        block = xs[:, width:].astype(F32)
        chosen = (wide_lane == me) | (wide_lane == me + experts)
        return jnp.sum(jnp.where(chosen, block, 0.0), axis=1, keepdims=True)

    def forward():
        projected = jnp.dot(xs[:, :width], wgu[...], preferred_element_type=F32)
        gate = projected[:, :ff]
        upward = projected[:, ff:]
        hidden = (gate * jax.nn.sigmoid(gate) * upward).astype(BF16)
        gate_s[...] = gate
        up_s[...] = upward
        hid_s[...] = hidden
        weight = my_weight()

        @pl.loop(0, width // tile)
        def _(j):
            cols = pl.ds(pl.multiple_of(j * tile, tile), tile)
            out = jnp.dot(hid_s[...], wd[:, cols], preferred_element_type=F32)
            pm[:, cols] = (out * weight).astype(BF16)

    across = (((1,), (1,)), ((), ()))

    def backward():
        plain = lax.dot_general(cs[...], wd[...], across, preferred_element_type=F32)
        gate = gate_s[...]
        upward = up_s[...]
        grads = plain * my_weight()
        sig = jax.nn.sigmoid(gate)
        grad_gate = grads * upward * sig * (1.0 + gate * (1.0 - sig))
        grad_up = grads * gate * sig
        dots = jnp.sum(plain * hid_s[...].astype(F32), axis=1, keepdims=True)
        coarse = dots.astype(BF16).astype(F32)
        pb[:, width:] = jnp.where(
            wide_lane == me, coarse, jnp.where(wide_lane == me + experts, dots - coarse, 0.0)
        ).astype(BF16)
        pair_s[:, :ff] = grad_gate.astype(BF16)
        pair_s[:, ff:] = grad_up.astype(BF16)

        @pl.loop(0, width // tile)
        def _(j):
            cols = pl.ds(pl.multiple_of(j * tile, tile), tile)
            back = lax.dot_general(pair_s[...], wgu[cols, :], across, preferred_element_type=F32)
            pb[:, cols] = back.astype(BF16)

    parts, from_core = (pm, pb), (cr_m, cr_b)
    to_x, from_x = (xs_m, xs_b), (xr_m, xr_b)
    to_z, from_z = (zs_m, zs_b), (zr_m, zr_b)

    def core_copy(t, other):
        src = parts[t].at[pl.ds(column(1 - x if other else x, 1 - c), quarter)]
        q = 1 if other else 0
        return (src, from_core[t].at[q], core_send.at[t, q], core_recv.at[t, q], sibling)

    def core_go(t, other):
        go(*core_copy(t, other))

    def core_wait(t, other):
        remote(*core_copy(t, other)).wait_recv()

    def core_rows(zz):
        return pl.ds(pl.multiple_of(zz * tok, tok), tok)

    def x_copy(t, zz):
        return (to_x[t].at[zz], from_x[t].at[zz], x_send.at[t, zz], x_recv.at[t, zz], partner)

    order = far + [z]

    def send_x(t):
        core_wait(t, True)
        for zz in order:
            own = parts[t][rows(1 - x, c, zz), :].astype(F32)
            to_x[t][zz] = (own + from_core[t][1, core_rows(zz), :].astype(F32)).astype(BF16)
            go(*x_copy(t, zz))

    def joined(t, zz):
        own = parts[t][rows(x, c, zz), :].astype(F32)
        return own + from_core[t][0, core_rows(zz), :].astype(F32) + from_x[t][zz].astype(F32)

    def send_z(t):
        core_wait(t, False)
        for zz in far:
            remote(*x_copy(t, zz)).wait_recv()
            to_z[t][zz] = joined(t, zz).astype(BF16)
            go(to_z[t].at[zz], from_z[t].at[z], z_send.at[t, zz], z_recv.at[t, z], zdev(zz))

    def finish(t):
        remote(*x_copy(t, z)).wait_recv()
        total = joined(t, z)
        for zz in near:
            remote(
                to_z[t].at[zz], from_z[t].at[zz], z_send.at[t, zz], z_recv.at[t, zz], zdev(zz)
            ).wait_recv()
            total = total + from_z[t][zz].astype(F32)
        return total

    own_go(0)
    for s in range(1, n):
        pass_z(0, s)
        if s == 1:
            own_go(1)
        if s == 2:
            pass_z(1, 1)
    pass_x(0)
    for s in range(min(2, n - 1), n):
        pass_z(1, s)
    load_gu.wait()
    load_d.wait()
    await_sibling(0, False)
    await_sibling(0, True)
    forward()
    core_go(0, True)
    core_go(0, False)
    pass_x(1)
    send_x(0)
    await_sibling(1, False)
    await_sibling(1, True)
    backward()
    core_go(1, True)
    core_go(1, False)
    send_z(0)
    send_x(1)
    mixed_ref[...] = finish(0).astype(mixed_ref.dtype)
    send_z(1)
    total = finish(1)
    grad_ref[...] = total[:, :width].astype(grad_ref.dtype)
    dots = total[:, width:]
    place = lax.broadcasted_iota(jnp.int32, (tok, top), 1)
    picked = jnp.zeros((tok, top), F32)
    for k in range(top):
        value = jnp.sum(jnp.where(ids[:, k : k + 1] == lane_expert, dots, 0.0), axis=1, keepdims=True)
        picked = picked + jnp.where(place == k, value, 0.0)
    gcomb_ref[...] = picked.T
    for copy in sends:
        copy.wait_send()
    for cond, copy in maybe:
        pl.when(cond)(copy.wait_send)


def copy_kernel(mixed_ref, grad_ref, dots_ref, mixed_out, grad_out, dots_out, sem):
    copies = [
        pltpu.make_async_copy(mixed_ref, mixed_out, sem.at[0]),
        pltpu.make_async_copy(grad_ref, grad_out, sem.at[1]),
        pltpu.make_async_copy(dots_ref, dots_out, sem.at[2]),
    ]
    for copy in copies:
        copy.start()
    for copy in copies:
        copy.wait()


def dense_plan(tokens, cotangent, expert_ids, combine, w_gate_up, w_down):
    n = lax.axis_size("node")
    tok, width = tokens.shape
    top = expert_ids.shape[1]
    ff = w_down.shape[1]
    total = 4 * n * tok
    wide = width + LANES
    vmem = pl.BlockSpec(memory_space=pltpu.VMEM)
    hbm = pl.BlockSpec(memory_space=pl.ANY)
    dma = pltpu.SemaphoreType.DMA
    mixed, grads, dots = pl.pallas_call(
        functools.partial(dense_kernel, n),
        out_shape=(
            jax.ShapeDtypeStruct((tok, width), BF16),
            jax.ShapeDtypeStruct((tok, width), BF16),
            jax.ShapeDtypeStruct((top, tok), F32),
        ),
        in_specs=[hbm] * 6,
        out_specs=(vmem, vmem, vmem),
        scratch_shapes=[
            pltpu.VMEM((top, tok), jnp.int32),
            pltpu.VMEM((top, tok), F32),
            pltpu.VMEM((width, 2 * ff), BF16),
            pltpu.VMEM((ff, width), BF16),
            pltpu.VMEM((total, wide), BF16),
            pltpu.VMEM((total, width), BF16),
            pltpu.VMEM((total, width), BF16),
            pltpu.VMEM((total, wide), BF16),
            pltpu.VMEM((total, ff), F32),
            pltpu.VMEM((total, ff), F32),
            pltpu.VMEM((total, ff), BF16),
            pltpu.VMEM((total, 2 * ff), BF16),
            pltpu.VMEM((2, n * tok, width), BF16),
            pltpu.VMEM((2, n * tok, wide), BF16),
            pltpu.VMEM((n, tok, width), BF16),
            pltpu.VMEM((n, tok, wide), BF16),
            pltpu.VMEM((n, tok, width), BF16),
            pltpu.VMEM((n, tok, wide), BF16),
            pltpu.VMEM((n, tok, width), BF16),
            pltpu.VMEM((n, tok, wide), BF16),
            pltpu.VMEM((n, tok, width), BF16),
            pltpu.VMEM((n, tok, wide), BF16),
            dma((6,)),
            dma((2, 3)),
            dma((2, 4, n)),
            dma((2, 4, n)),
            dma((2, 2)),
            dma((2, 2)),
            dma((2, n)),
            dma((2, n)),
            dma((2, n)),
            dma((2, n)),
        ],
        compiler_params=pltpu.CompilerParams(
            collective_id=0, has_side_effects=True, vmem_limit_bytes=62 * 1024 * 1024
        ),
    )(tokens, cotangent, expert_ids.T, combine.T, w_gate_up, w_down)
    mixed, grads, dots = pl.pallas_call(
        copy_kernel,
        out_shape=tuple(jax.ShapeDtypeStruct(a.shape, a.dtype) for a in (mixed, grads, dots)),
        in_specs=[hbm] * 3,
        out_specs=(hbm,) * 3,
        scratch_shapes=[dma((3,))],
        compiler_params=pltpu.CompilerParams(vmem_limit_bytes=62 * 1024 * 1024),
    )(mixed, grads, dots)
    return mixed, grads, dots.T


def choose_plan(tokens, cotangent, expert_ids, combine, w_gate_up, w_down):
    local_count = lax.axis_size("local")
    experts = lax.axis_size("node") * local_count
    tok_rows, top_count = expert_ids.shape
    capacity = max(2, 2 * tok_rows * top_count // experts)
    dense = capacity >= tok_rows and local_count == 4 and 2 * experts <= LANES and tok_rows % 16 == 0
    plan = dense_plan if dense else per_device
    return plan(tokens, cotangent, expert_ids, combine, w_gate_up, w_down)


def solution(mesh):
    placed = (
        P(("dp", "node", "local"), None),
        P(("dp", "node", "local"), None),
        P(("dp", "node", "local"), None),
        P(("dp", "node", "local"), None),
        P(("node", "local"), None, None),
        P(("node", "local"), None, None),
    )
    return jax.shard_map(
        choose_plan,
        mesh=mesh,
        in_specs=placed,
        out_specs=(
            P(("dp", "node", "local"), None),
            P(("dp", "node", "local"), None),
            P(("dp", "node", "local"), None),
        ),
        check_vma=False,
    )
```

```python
import functools

import jax
import jax.numpy as jnp
from jax import lax
from jax.experimental import pallas as pl
from jax.experimental.pallas import tpu as pltpu
from jax.sharding import PartitionSpec as P

MESH = pl.DeviceIdType.MESH
LANES = 128
F32 = jnp.float32
BF16 = jnp.bfloat16


def expert_forward(rows, w_gate_up, w_down):
    width = w_down.shape[0]
    projected = jnp.dot(rows, w_gate_up, preferred_element_type=jnp.float32)
    gate = projected[:, :width]
    upward = projected[:, width:]
    hidden = (gate * jax.nn.sigmoid(gate) * upward).astype(jnp.bfloat16)
    output = jnp.dot(hidden, w_down, preferred_element_type=jnp.float32).astype(jnp.bfloat16)
    return (output, gate, upward)


def expert_backward(grads, gate, upward, w_gate_up, w_down):
    grad_hidden = lax.dot_general(
        grads, w_down, (((1,), (1,)), ((), ())), preferred_element_type=jnp.float32
    )
    sigmoid = jax.nn.sigmoid(gate)
    grad_gate = grad_hidden * upward * sigmoid * (1.0 + gate * (1.0 - sigmoid))
    grad_up = grad_hidden * gate * sigmoid
    paired = jnp.concatenate([grad_gate, grad_up], axis=1).astype(jnp.bfloat16)
    back = lax.dot_general(
        paired, w_gate_up, (((1,), (1,)), ((), ())), preferred_element_type=jnp.float32
    )
    return back.astype(jnp.bfloat16)


def node_tables(ids_all, weights_all, node_here, node_count, local_count, capacity):
    rows_all, top_count = ids_all.shape
    tok_rows = rows_all // node_count
    experts = node_count * local_count
    per_source = ids_all.reshape(node_count, tok_rows * top_count)
    onehot = (per_source[:, :, None] == jnp.arange(experts, dtype=jnp.int32)[None, None, :]).astype(
        jnp.int32
    )
    before = jnp.cumsum(onehot, axis=1) - onehot
    ranks = jnp.sum(before * onehot, axis=2)
    source = jnp.arange(node_count, dtype=jnp.int32)[:, None]
    inside = per_source // local_count == node_here
    slots = per_source % local_count * (node_count * capacity) + source * capacity + ranks
    slots = jnp.where(inside, slots, -1).reshape(rows_all, top_count)
    matches = (
        slots[None, :, :]
        == jnp.arange(local_count * node_count * capacity, dtype=jnp.int32)[:, None, None]
    )
    placing = jnp.any(matches, axis=2).astype(jnp.bfloat16)
    slot_weight = jnp.sum(jnp.where(matches, weights_all[None, :, :], 0.0), axis=(1, 2))
    return (matches, placing, slot_weight)


def per_device(tokens, cotangent, expert_ids, combine, w_gate_up, w_down):
    node_count = lax.axis_size("node")
    local_count = lax.axis_size("local")
    experts = node_count * local_count
    tok_rows, top_count = expert_ids.shape
    width = tokens.shape[1]
    capacity = max(2, 2 * tok_rows * top_count // experts)
    gate_up_one = w_gate_up[0]
    down_one = w_down[0]
    route = jnp.concatenate([expert_ids.astype(jnp.float32), combine], axis=1)
    route_all = lax.all_gather(route, "node", axis=0, tiled=True)
    ids_all = route_all[:, :top_count].astype(jnp.int32)
    weights_all = route_all[:, top_count:]
    tokens_all, cot_all = (
        lax.all_gather(tokens, "node", axis=0, tiled=True),
        lax.all_gather(cotangent, "node", axis=0, tiled=True),
    )
    matches, placing, slot_weight = node_tables(
        ids_all, weights_all, lax.axis_index("node"), node_count, local_count, capacity
    )
    send_x = jnp.dot(placing, tokens_all, preferred_element_type=jnp.float32).astype(jnp.bfloat16)
    send_x = send_x.reshape(local_count, node_count * capacity, width)
    cot_rows = jnp.dot(placing, cot_all, preferred_element_type=jnp.float32)
    send_g = (cot_rows * slot_weight[:, None]).astype(jnp.bfloat16)
    send_g = send_g.reshape(local_count, node_count * capacity, width)
    arrived, arrived_grad = (
        lax.all_to_all(send_x, "local", split_axis=0, concat_axis=0, tiled=True),
        lax.all_to_all(send_g, "local", split_axis=0, concat_axis=0, tiled=True),
    )
    output, gate, upward = expert_forward(arrived.reshape(-1, width), gate_up_one, down_one)
    back = expert_backward(arrived_grad.reshape(-1, width), gate, upward, gate_up_one, down_one)
    output = output.reshape(local_count, node_count * capacity, width)
    back = back.reshape(local_count, node_count * capacity, width)
    came_back, back_home = (
        lax.all_to_all(output, "local", split_axis=0, concat_axis=0, tiled=True),
        lax.all_to_all(back, "local", split_axis=0, concat_axis=0, tiled=True),
    )
    flat_out = came_back.reshape(-1, width).astype(jnp.float32)
    flat_back = back_home.reshape(-1, width)
    gather_rows = placing.T
    mixed_part = jnp.dot(
        gather_rows.astype(jnp.float32),
        flat_out * slot_weight[:, None],
        precision=lax.Precision.HIGHEST,
    )
    back_part = jnp.dot(gather_rows, flat_back, preferred_element_type=jnp.float32)
    slot_dot = jnp.sum(cot_rows * flat_out, axis=1)
    combine_part = jnp.sum(jnp.where(matches, slot_dot[:, None, None], 0.0), axis=0)
    mixed, grad_tokens, grad_combine = (
        lax.psum_scatter(mixed_part, "node", scatter_dimension=0, tiled=True),
        lax.psum_scatter(back_part, "node", scatter_dimension=0, tiled=True),
        lax.psum_scatter(combine_part, "node", scatter_dimension=0, tiled=True),
    )
    return (mixed.astype(jnp.bfloat16), grad_tokens.astype(jnp.bfloat16), grad_combine)


def dense_kernel(
    n,
    tok_hbm,
    cot_hbm,
    ids_hbm,
    comb_hbm,
    gate_up_hbm,
    down_hbm,
    mixed_ref,
    grad_ref,
    gcomb_ref,
    ids_t,
    comb_t,
    wgu,
    wd,
    xs,
    cs,
    pm,
    pb,
    gate_s,
    up_s,
    hid_s,
    pair_s,
    cr_m,
    cr_b,
    xs_m,
    xs_b,
    xr_m,
    xr_b,
    zs_m,
    zs_b,
    zr_m,
    zr_b,
    w_sem,
    nd_send,
    ag_send,
    ag_recv,
    core_send,
    core_recv,
    x_send,
    x_recv,
    z_send,
    z_recv,
):
    tok, width = tok_hbm.shape
    top = ids_hbm.shape[0]
    ff = wd.shape[0]
    z = lax.axis_index("node")
    local = lax.axis_index("local")
    x, c = local // 2, local % 2
    experts = n * 4
    me = z * 4 + local
    half = 2 * n * tok
    quarter = n * tok

    partner = {"local": (1 - x) * 2 + c}
    sibling = {"local": x * 2 + 1 - c}

    reach = jnp.minimum(z, n - 1 - z)
    toward = jnp.where(z < n - 1 - z, 1, -1)
    near = []
    for s in range(1, n):
        turn = (s + 1) // 2 * (1 if s % 2 else -1)
        near.append(z + toward * jnp.where(s <= 2 * reach, turn, s - reach))
    far = near[::-1]

    def zdev(zz):
        return {"node": zz}

    def column(xx, cc):
        return pl.multiple_of((xx * 2 + cc) * quarter, quarter)

    def rows(xx, cc, zz):
        return pl.ds(pl.multiple_of(((xx * 2 + cc) * n + zz) * tok, tok), tok)

    mine = rows(x, c, z)
    load_own = [
        pltpu.make_async_copy(ids_hbm, ids_t, w_sem.at[2]),
        pltpu.make_async_copy(comb_hbm, comb_t, w_sem.at[3]),
        pltpu.make_async_copy(tok_hbm, xs.at[mine, pl.ds(0, width)], w_sem.at[4]),
        pltpu.make_async_copy(cot_hbm, cs.at[mine], w_sem.at[5]),
    ]
    for copy in load_own:
        copy.start()
    load_gu = pltpu.make_async_copy(gate_up_hbm.at[0], wgu, w_sem.at[0])
    load_d = pltpu.make_async_copy(down_hbm.at[0], wd, w_sem.at[1])
    load_gu.start()
    load_d.start()

    barrier = pltpu.get_barrier_semaphore()
    for zz in near:
        pl.semaphore_signal(barrier, inc=1, device_id=zdev(zz), device_id_type=MESH)
    pl.semaphore_signal(barrier, inc=1, device_id=partner, device_id_type=MESH)
    pl.semaphore_signal(barrier, inc=1, device_id=sibling, device_id_type=MESH)

    for copy in load_own:
        copy.wait()
    lane = lax.broadcasted_iota(jnp.int32, (tok, LANES), 1)
    lane_expert = jnp.where(lane < experts, lane, lane - experts)
    ids = ids_t[...].T
    comb = comb_t[...].T
    weight = jnp.zeros((tok, LANES), F32)
    for k in range(top):
        weight = weight + jnp.where(ids[:, k : k + 1] == lane_expert, comb[:, k : k + 1], 0.0)
    coarse = weight.astype(BF16).astype(F32)
    xs[mine, width:] = jnp.where(lane < experts, coarse, weight - coarse).astype(BF16)
    pl.semaphore_wait(barrier, n + 1)

    sends = []
    maybe = []

    def remote(src, dst, send_sem, recv_sem, device):
        return pltpu.make_async_remote_copy(
            src_ref=src,
            dst_ref=dst,
            send_sem=send_sem,
            recv_sem=recv_sem,
            device_id=device,
            device_id_type=MESH,
        )

    def go(*args):
        copy = remote(*args)
        copy.start()
        sends.append(copy)

    bufs = (xs, cs)

    def gather_go(t, role, zz, where, device):
        go(bufs[t].at[where], bufs[t].at[where], ag_send.at[t, role, zz], ag_recv.at[t, role, zz], device)

    def gather_wait(t, role, zz, where):
        remote(
            bufs[t].at[where], bufs[t].at[where], ag_send.at[t, role, zz], ag_recv.at[t, role, zz], sibling
        ).wait_recv()

    def inside(zz):
        return (zz >= 0) & (zz < n)

    def go_if(cond, *args):
        copy = remote(*args)
        pl.when(cond)(copy.start)
        maybe.append((cond, copy))

    def own_go(t):
        for i, to in enumerate((z - 1, z + 1)):
            device = zdev(jnp.clip(to, 0, n - 1))
            block = bufs[t].at[mine]
            go_if(inside(to), block, block, nd_send.at[t, i], ag_recv.at[t, 0, z], device)
        gather_go(t, 1, z, mine, partner)
        gather_go(t, 2, z, mine, sibling)

    def pass_z(t, s):
        for side in (-1, 1):
            here = inside(z + side * s)
            zz = jnp.clip(z + side * s, 0, n - 1)
            to = z - side
            where = rows(x, c, zz)
            block = bufs[t].at[where]
            pl.when(here)(functools.partial(gather_wait, t, 0, zz, where))
            if s < n - 1:
                device = zdev(jnp.clip(to, 0, n - 1))
                go_if(here & inside(to), block, block, ag_send.at[t, 0, zz], ag_recv.at[t, 0, zz], device)
            go_if(here, block, block, ag_send.at[t, 1, zz], ag_recv.at[t, 1, zz], partner)
            go_if(here, block, block, ag_send.at[t, 2, zz], ag_recv.at[t, 2, zz], sibling)

    def pass_x(t, places):
        for zz in places:
            where = rows(1 - x, c, zz)
            gather_wait(t, 1, zz, where)
            gather_go(t, 3, zz, where, sibling)

    def await_sibling(t, other):
        for zz in [z] + near:
            where = rows(1 - x if other else x, 1 - c, zz)
            gather_wait(t, 3 if other else 2, zz, where)

    tile = 512 if width % 512 == 0 else width
    total_rows = 2 * half
    wide_lane = lax.broadcasted_iota(jnp.int32, (total_rows, LANES), 1)

    def my_weight():
        block = xs[:, width:].astype(F32)
        chosen = (wide_lane == me) | (wide_lane == me + experts)
        return jnp.sum(jnp.where(chosen, block, 0.0), axis=1, keepdims=True)

    def forward_hidden():
        projected = jnp.dot(xs[:, :width], wgu[...], preferred_element_type=F32)
        gate = projected[:, :ff]
        upward = projected[:, ff:]
        hidden = (gate * jax.nn.sigmoid(gate) * upward).astype(BF16)
        gate_s[...] = gate
        up_s[...] = upward
        hid_s[...] = hidden

    def forward_out():
        weight = my_weight()

        @pl.loop(0, width // tile)
        def _(j):
            cols = pl.ds(pl.multiple_of(j * tile, tile), tile)
            out = jnp.dot(hid_s[...], wd[:, cols], preferred_element_type=F32)
            pm[:, cols] = (out * weight).astype(BF16)

    across = (((1,), (1,)), ((), ()))

    def backward_hidden():
        plain = lax.dot_general(cs[...], wd[...], across, preferred_element_type=F32)
        gate = gate_s[...]
        upward = up_s[...]
        grads = plain * my_weight()
        sig = jax.nn.sigmoid(gate)
        grad_gate = grads * upward * sig * (1.0 + gate * (1.0 - sig))
        grad_up = grads * gate * sig
        dots = jnp.sum(plain * hid_s[...].astype(F32), axis=1, keepdims=True)
        coarse = dots.astype(BF16).astype(F32)
        pb[:, width:] = jnp.where(
            wide_lane == me, coarse, jnp.where(wide_lane == me + experts, dots - coarse, 0.0)
        ).astype(BF16)
        pair_s[:, :ff] = grad_gate.astype(BF16)
        pair_s[:, ff:] = grad_up.astype(BF16)

    def backward_out():
        @pl.loop(0, width // tile)
        def _(j):
            cols = pl.ds(pl.multiple_of(j * tile, tile), tile)
            back = lax.dot_general(pair_s[...], wgu[cols, :], across, preferred_element_type=F32)
            pb[:, cols] = back.astype(BF16)

    parts, from_core = (pm, pb), (cr_m, cr_b)
    to_x, from_x = (xs_m, xs_b), (xr_m, xr_b)
    to_z, from_z = (zs_m, zs_b), (zr_m, zr_b)

    def core_copy(t, other):
        src = parts[t].at[pl.ds(column(1 - x if other else x, 1 - c), quarter)]
        q = 1 if other else 0
        return (src, from_core[t].at[q], core_send.at[t, q], core_recv.at[t, q], sibling)

    def core_go(t, other):
        go(*core_copy(t, other))

    def core_wait(t, other):
        remote(*core_copy(t, other)).wait_recv()

    def core_rows(zz):
        return pl.ds(pl.multiple_of(zz * tok, tok), tok)

    def x_copy(t, zz):
        return (to_x[t].at[zz], from_x[t].at[zz], x_send.at[t, zz], x_recv.at[t, zz], partner)

    order = far + [z]

    def send_x(t):
        started = []
        core_wait(t, True)
        for i, zz in enumerate(order):
            own = parts[t][rows(1 - x, c, zz), :].astype(F32)
            to_x[t][zz] = (own + from_core[t][1, core_rows(zz), :].astype(F32)).astype(BF16)
            copy = remote(*x_copy(t, zz))
            copy.start()
            started.append(copy)
            if t == 1 and i >= 1:
                started[i - 1].wait_send()
        sends.extend(started if t == 0 else started[-1:])

    def joined(t, zz):
        own = parts[t][rows(x, c, zz), :].astype(F32)
        return own + from_core[t][0, core_rows(zz), :].astype(F32) + from_x[t][zz].astype(F32)

    def send_z(t):
        core_wait(t, False)
        for zz in far:
            remote(*x_copy(t, zz)).wait_recv()
            to_z[t][zz] = joined(t, zz).astype(BF16)
            go(to_z[t].at[zz], from_z[t].at[z], z_send.at[t, zz], z_recv.at[t, z], zdev(zz))

    def finish(t):
        remote(*x_copy(t, z)).wait_recv()
        total = joined(t, z)
        for zz in near:
            remote(
                to_z[t].at[zz], from_z[t].at[zz], z_send.at[t, zz], z_recv.at[t, zz], zdev(zz)
            ).wait_recv()
            total = total + from_z[t][zz].astype(F32)
        return total

    own_go(0)
    for s in range(1, n):
        pass_z(0, s)
        if s == 1:
            own_go(1)
        if s == 2:
            pass_z(1, 1)
    pass_x(0, [z] + near)
    load_gu.wait()
    load_d.wait()
    await_sibling(0, False)
    await_sibling(0, True)
    forward_hidden()
    for s in range(min(2, n - 1), n):
        pass_z(1, s)
    forward_out()
    core_go(0, True)
    core_go(0, False)
    pass_x(1, [z] + near[:1])
    send_x(0)
    pass_x(1, near[1:])
    await_sibling(1, False)
    await_sibling(1, True)
    backward_hidden()
    send_z(0)
    backward_out()
    core_go(1, True)
    core_go(1, False)
    send_x(1)
    mixed_ref[...] = finish(0).astype(mixed_ref.dtype)
    send_z(1)
    total = finish(1)
    grad_ref[...] = total[:, :width].astype(grad_ref.dtype)
    dots = total[:, width:]
    place = lax.broadcasted_iota(jnp.int32, (tok, top), 1)
    picked = jnp.zeros((tok, top), F32)
    for k in range(top):
        value = jnp.sum(jnp.where(ids[:, k : k + 1] == lane_expert, dots, 0.0), axis=1, keepdims=True)
        picked = picked + jnp.where(place == k, value, 0.0)
    gcomb_ref[...] = picked.T
    for copy in sends:
        copy.wait_send()
    for cond, copy in maybe:
        pl.when(cond)(copy.wait_send)


def dense_plan(tokens, cotangent, expert_ids, combine, w_gate_up, w_down):
    n = lax.axis_size("node")
    tok, width = tokens.shape
    top = expert_ids.shape[1]
    ff = w_down.shape[1]
    total = 4 * n * tok
    wide = width + LANES
    vmem = pl.BlockSpec(memory_space=pltpu.VMEM)
    hbm = pl.BlockSpec(memory_space=pl.ANY)
    dma = pltpu.SemaphoreType.DMA
    mixed, grads, dots = pl.pallas_call(
        functools.partial(dense_kernel, n),
        out_shape=(
            jax.ShapeDtypeStruct((tok, width), BF16),
            jax.ShapeDtypeStruct((tok, width), BF16),
            jax.ShapeDtypeStruct((top, tok), F32),
        ),
        in_specs=[hbm] * 6,
        out_specs=(vmem, vmem, vmem),
        scratch_shapes=[
            pltpu.VMEM((top, tok), jnp.int32),
            pltpu.VMEM((top, tok), F32),
            pltpu.VMEM((width, 2 * ff), BF16),
            pltpu.VMEM((ff, width), BF16),
            pltpu.VMEM((total, wide), BF16),
            pltpu.VMEM((total, width), BF16),
            pltpu.VMEM((total, width), BF16),
            pltpu.VMEM((total, wide), BF16),
            pltpu.VMEM((total, ff), F32),
            pltpu.VMEM((total, ff), F32),
            pltpu.VMEM((total, ff), BF16),
            pltpu.VMEM((total, 2 * ff), BF16),
            pltpu.VMEM((2, n * tok, width), BF16),
            pltpu.VMEM((2, n * tok, wide), BF16),
            pltpu.VMEM((n, tok, width), BF16),
            pltpu.VMEM((n, tok, wide), BF16),
            pltpu.VMEM((n, tok, width), BF16),
            pltpu.VMEM((n, tok, wide), BF16),
            pltpu.VMEM((n, tok, width), BF16),
            pltpu.VMEM((n, tok, wide), BF16),
            pltpu.VMEM((n, tok, width), BF16),
            pltpu.VMEM((n, tok, wide), BF16),
            dma((6,)),
            dma((2, n)),
            dma((2, 4, n)),
            dma((2, 4, n)),
            dma((2, 2)),
            dma((2, 2)),
            dma((2, n)),
            dma((2, n)),
            dma((2, n)),
            dma((2, n)),
        ],
        compiler_params=pltpu.CompilerParams(
            collective_id=0, has_side_effects=True, vmem_limit_bytes=62 * 1024 * 1024
        ),
    )(tokens, cotangent, expert_ids.T, combine.T, w_gate_up, w_down)
    return mixed, grads, dots.T


def choose_plan(tokens, cotangent, expert_ids, combine, w_gate_up, w_down):
    local_count = lax.axis_size("local")
    experts = lax.axis_size("node") * local_count
    tok_rows, top_count = expert_ids.shape
    capacity = max(2, 2 * tok_rows * top_count // experts)
    dense = capacity >= tok_rows and local_count == 4 and 2 * experts <= LANES and tok_rows % 16 == 0
    plan = dense_plan if dense else per_device
    return plan(tokens, cotangent, expert_ids, combine, w_gate_up, w_down)


def solution(mesh):
    placed = (
        P(("dp", "node", "local"), None),
        P(("dp", "node", "local"), None),
        P(("dp", "node", "local"), None),
        P(("dp", "node", "local"), None),
        P(("node", "local"), None, None),
        P(("node", "local"), None, None),
    )
    return jax.shard_map(
        choose_plan,
        mesh=mesh,
        in_specs=placed,
        out_specs=(
            P(("dp", "node", "local"), None),
            P(("dp", "node", "local"), None),
            P(("dp", "node", "local"), None),
        ),
        check_vma=False,
    )
```

```python
import functools

import jax
import jax.numpy as jnp
from jax import lax
from jax.experimental import pallas as pl
from jax.experimental.pallas import tpu as pltpu
from jax.sharding import PartitionSpec as P

MESH = pl.DeviceIdType.MESH
LANES = 128
F32 = jnp.float32
BF16 = jnp.bfloat16


def expert_forward(rows, w_gate_up, w_down):
    width = w_down.shape[0]
    projected = jnp.dot(rows, w_gate_up, preferred_element_type=jnp.float32)
    gate = projected[:, :width]
    upward = projected[:, width:]
    hidden = (gate * jax.nn.sigmoid(gate) * upward).astype(jnp.bfloat16)
    output = jnp.dot(hidden, w_down, preferred_element_type=jnp.float32).astype(jnp.bfloat16)
    return (output, gate, upward)


def expert_backward(grads, gate, upward, w_gate_up, w_down):
    grad_hidden = lax.dot_general(
        grads, w_down, (((1,), (1,)), ((), ())), preferred_element_type=jnp.float32
    )
    sigmoid = jax.nn.sigmoid(gate)
    grad_gate = grad_hidden * upward * sigmoid * (1.0 + gate * (1.0 - sigmoid))
    grad_up = grad_hidden * gate * sigmoid
    paired = jnp.concatenate([grad_gate, grad_up], axis=1).astype(jnp.bfloat16)
    back = lax.dot_general(
        paired, w_gate_up, (((1,), (1,)), ((), ())), preferred_element_type=jnp.float32
    )
    return back.astype(jnp.bfloat16)


def node_tables(ids_all, weights_all, node_here, node_count, local_count, capacity):
    rows_all, top_count = ids_all.shape
    tok_rows = rows_all // node_count
    experts = node_count * local_count
    per_source = ids_all.reshape(node_count, tok_rows * top_count)
    onehot = (per_source[:, :, None] == jnp.arange(experts, dtype=jnp.int32)[None, None, :]).astype(
        jnp.int32
    )
    before = jnp.cumsum(onehot, axis=1) - onehot
    ranks = jnp.sum(before * onehot, axis=2)
    source = jnp.arange(node_count, dtype=jnp.int32)[:, None]
    inside = per_source // local_count == node_here
    slots = per_source % local_count * (node_count * capacity) + source * capacity + ranks
    slots = jnp.where(inside, slots, -1).reshape(rows_all, top_count)
    matches = (
        slots[None, :, :]
        == jnp.arange(local_count * node_count * capacity, dtype=jnp.int32)[:, None, None]
    )
    placing = jnp.any(matches, axis=2).astype(jnp.bfloat16)
    slot_weight = jnp.sum(jnp.where(matches, weights_all[None, :, :], 0.0), axis=(1, 2))
    return (matches, placing, slot_weight)


def per_device(tokens, cotangent, expert_ids, combine, w_gate_up, w_down):
    node_count = lax.axis_size("node")
    local_count = lax.axis_size("local")
    experts = node_count * local_count
    tok_rows, top_count = expert_ids.shape
    width = tokens.shape[1]
    capacity = max(2, 2 * tok_rows * top_count // experts)
    gate_up_one = w_gate_up[0]
    down_one = w_down[0]
    route = jnp.concatenate([expert_ids.astype(jnp.float32), combine], axis=1)
    route_all = lax.all_gather(route, "node", axis=0, tiled=True)
    ids_all = route_all[:, :top_count].astype(jnp.int32)
    weights_all = route_all[:, top_count:]
    tokens_all, cot_all = (
        lax.all_gather(tokens, "node", axis=0, tiled=True),
        lax.all_gather(cotangent, "node", axis=0, tiled=True),
    )
    matches, placing, slot_weight = node_tables(
        ids_all, weights_all, lax.axis_index("node"), node_count, local_count, capacity
    )
    send_x = jnp.dot(placing, tokens_all, preferred_element_type=jnp.float32).astype(jnp.bfloat16)
    send_x = send_x.reshape(local_count, node_count * capacity, width)
    cot_rows = jnp.dot(placing, cot_all, preferred_element_type=jnp.float32)
    send_g = (cot_rows * slot_weight[:, None]).astype(jnp.bfloat16)
    send_g = send_g.reshape(local_count, node_count * capacity, width)
    arrived, arrived_grad = (
        lax.all_to_all(send_x, "local", split_axis=0, concat_axis=0, tiled=True),
        lax.all_to_all(send_g, "local", split_axis=0, concat_axis=0, tiled=True),
    )
    output, gate, upward = expert_forward(arrived.reshape(-1, width), gate_up_one, down_one)
    back = expert_backward(arrived_grad.reshape(-1, width), gate, upward, gate_up_one, down_one)
    output = output.reshape(local_count, node_count * capacity, width)
    back = back.reshape(local_count, node_count * capacity, width)
    came_back, back_home = (
        lax.all_to_all(output, "local", split_axis=0, concat_axis=0, tiled=True),
        lax.all_to_all(back, "local", split_axis=0, concat_axis=0, tiled=True),
    )
    flat_out = came_back.reshape(-1, width).astype(jnp.float32)
    flat_back = back_home.reshape(-1, width)
    gather_rows = placing.T
    mixed_part = jnp.dot(
        gather_rows.astype(jnp.float32),
        flat_out * slot_weight[:, None],
        precision=lax.Precision.HIGHEST,
    )
    back_part = jnp.dot(gather_rows, flat_back, preferred_element_type=jnp.float32)
    slot_dot = jnp.sum(cot_rows * flat_out, axis=1)
    combine_part = jnp.sum(jnp.where(matches, slot_dot[:, None, None], 0.0), axis=0)
    mixed, grad_tokens, grad_combine = (
        lax.psum_scatter(mixed_part, "node", scatter_dimension=0, tiled=True),
        lax.psum_scatter(back_part, "node", scatter_dimension=0, tiled=True),
        lax.psum_scatter(combine_part, "node", scatter_dimension=0, tiled=True),
    )
    return (mixed.astype(jnp.bfloat16), grad_tokens.astype(jnp.bfloat16), grad_combine)


def dense_kernel(
    n,
    tok_hbm,
    cot_hbm,
    ids_hbm,
    comb_hbm,
    gate_up_hbm,
    down_hbm,
    mixed_ref,
    grad_ref,
    gcomb_ref,
    ids_t,
    comb_t,
    wgu,
    wd,
    xs,
    cs,
    pm,
    pb,
    gate_s,
    up_s,
    hid_s,
    pair_s,
    cr_m,
    cr_b,
    xs_m,
    xs_b,
    xr_m,
    xr_b,
    zs_m,
    zs_b,
    zr_m,
    zr_b,
    w_sem,
    nd_send,
    ag_send,
    ag_recv,
    core_send,
    core_recv,
    x_send,
    x_recv,
    z_send,
    z_recv,
):
    tok, width = tok_hbm.shape
    top = ids_hbm.shape[0]
    ff = wd.shape[0]
    z = lax.axis_index("node")
    local = lax.axis_index("local")
    x, c = local // 2, local % 2
    experts = n * 4
    me = z * 4 + local
    half = 2 * n * tok
    quarter = n * tok

    partner = {"local": (1 - x) * 2 + c}
    sibling = {"local": x * 2 + 1 - c}

    reach = jnp.minimum(z, n - 1 - z)
    toward = jnp.where(z < n - 1 - z, 1, -1)
    near = []
    for s in range(1, n):
        turn = (s + 1) // 2 * (1 if s % 2 else -1)
        near.append(z + toward * jnp.where(s <= 2 * reach, turn, s - reach))
    far = near[::-1]

    def zdev(zz):
        return {"node": zz}

    def column(xx, cc):
        return pl.multiple_of((xx * 2 + cc) * quarter, quarter)

    def rows(xx, cc, zz):
        return pl.ds(pl.multiple_of(((xx * 2 + cc) * n + zz) * tok, tok), tok)

    mine = rows(x, c, z)
    load_own = [
        pltpu.make_async_copy(ids_hbm, ids_t, w_sem.at[2]),
        pltpu.make_async_copy(comb_hbm, comb_t, w_sem.at[3]),
        pltpu.make_async_copy(tok_hbm, xs.at[mine, pl.ds(0, width)], w_sem.at[4]),
        pltpu.make_async_copy(cot_hbm, cs.at[mine], w_sem.at[5]),
    ]
    for copy in load_own:
        copy.start()
    load_gu = pltpu.make_async_copy(gate_up_hbm.at[0], wgu, w_sem.at[0])
    load_d = pltpu.make_async_copy(down_hbm.at[0], wd, w_sem.at[1])
    load_gu.start()
    load_d.start()

    barrier = pltpu.get_barrier_semaphore()
    for zz in near:
        pl.semaphore_signal(barrier, inc=1, device_id=zdev(zz), device_id_type=MESH)
    pl.semaphore_signal(barrier, inc=1, device_id=partner, device_id_type=MESH)
    pl.semaphore_signal(barrier, inc=1, device_id=sibling, device_id_type=MESH)

    for copy in load_own:
        copy.wait()
    lane = lax.broadcasted_iota(jnp.int32, (tok, LANES), 1)
    lane_expert = jnp.where(lane < experts, lane, lane - experts)
    ids = ids_t[...].T
    comb = comb_t[...].T
    weight = jnp.zeros((tok, LANES), F32)
    for k in range(top):
        weight = weight + jnp.where(ids[:, k : k + 1] == lane_expert, comb[:, k : k + 1], 0.0)
    coarse = weight.astype(BF16).astype(F32)
    xs[mine, width:] = jnp.where(lane < experts, coarse, weight - coarse).astype(BF16)
    pl.semaphore_wait(barrier, n + 1)

    sends = []
    maybe = []

    def remote(src, dst, send_sem, recv_sem, device):
        return pltpu.make_async_remote_copy(
            src_ref=src,
            dst_ref=dst,
            send_sem=send_sem,
            recv_sem=recv_sem,
            device_id=device,
            device_id_type=MESH,
        )

    def go(*args):
        copy = remote(*args)
        copy.start()
        sends.append(copy)

    bufs = (xs, cs)

    def gather_go(t, role, zz, where, device):
        go(bufs[t].at[where], bufs[t].at[where], ag_send.at[t, role, zz], ag_recv.at[t, role, zz], device)

    def gather_wait(t, role, zz, where):
        remote(
            bufs[t].at[where], bufs[t].at[where], ag_send.at[t, role, zz], ag_recv.at[t, role, zz], sibling
        ).wait_recv()

    def inside(zz):
        return (zz >= 0) & (zz < n)

    def go_if(cond, *args):
        copy = remote(*args)
        pl.when(cond)(copy.start)
        maybe.append((cond, copy))

    def own_go(t):
        for i, to in enumerate((z - 1, z + 1)):
            device = zdev(jnp.clip(to, 0, n - 1))
            block = bufs[t].at[mine]
            go_if(inside(to), block, block, nd_send.at[t, i], ag_recv.at[t, 0, z], device)
        gather_go(t, 1, z, mine, partner)
        gather_go(t, 2, z, mine, sibling)

    def pass_z(t, s):
        for side in (-1, 1):
            here = inside(z + side * s)
            zz = jnp.clip(z + side * s, 0, n - 1)
            to = z - side
            where = rows(x, c, zz)
            block = bufs[t].at[where]
            pl.when(here)(functools.partial(gather_wait, t, 0, zz, where))
            if s < n - 1:
                device = zdev(jnp.clip(to, 0, n - 1))
                go_if(here & inside(to), block, block, ag_send.at[t, 0, zz], ag_recv.at[t, 0, zz], device)
            go_if(here, block, block, ag_send.at[t, 1, zz], ag_recv.at[t, 1, zz], partner)
            go_if(here, block, block, ag_send.at[t, 2, zz], ag_recv.at[t, 2, zz], sibling)

    def pass_x(t, places):
        for zz in places:
            where = rows(1 - x, c, zz)
            gather_wait(t, 1, zz, where)
            gather_go(t, 3, zz, where, sibling)

    def await_sibling(t, other):
        for zz in [z] + near:
            where = rows(1 - x if other else x, 1 - c, zz)
            gather_wait(t, 3 if other else 2, zz, where)

    tile = 512 if width % 512 == 0 else width
    total_rows = 2 * half
    wide_lane = lax.broadcasted_iota(jnp.int32, (total_rows, LANES), 1)

    def my_weight():
        block = xs[:, width:].astype(F32)
        chosen = (wide_lane == me) | (wide_lane == me + experts)
        return jnp.sum(jnp.where(chosen, block, 0.0), axis=1, keepdims=True)

    def forward_hidden():
        projected = jnp.dot(xs[:, :width], wgu[...], preferred_element_type=F32)
        gate = projected[:, :ff]
        upward = projected[:, ff:]
        hidden = (gate * jax.nn.sigmoid(gate) * upward).astype(BF16)
        gate_s[...] = gate
        up_s[...] = upward
        hid_s[...] = hidden

    def forward_out():
        weight = my_weight()

        @pl.loop(0, width // tile)
        def _(j):
            cols = pl.ds(pl.multiple_of(j * tile, tile), tile)
            out = jnp.dot(hid_s[...], wd[:, cols], preferred_element_type=F32)
            pm[:, cols] = (out * weight).astype(BF16)

    across = (((1,), (1,)), ((), ()))

    def backward_hidden():
        plain = lax.dot_general(cs[...], wd[...], across, preferred_element_type=F32)
        gate = gate_s[...]
        upward = up_s[...]
        grads = plain * my_weight()
        sig = jax.nn.sigmoid(gate)
        grad_gate = grads * upward * sig * (1.0 + gate * (1.0 - sig))
        grad_up = grads * gate * sig
        dots = jnp.sum(plain * hid_s[...].astype(F32), axis=1, keepdims=True)
        coarse = dots.astype(BF16).astype(F32)
        pb[:, width:] = jnp.where(
            wide_lane == me, coarse, jnp.where(wide_lane == me + experts, dots - coarse, 0.0)
        ).astype(BF16)
        pair_s[:, :ff] = grad_gate.astype(BF16)
        pair_s[:, ff:] = grad_up.astype(BF16)

    def backward_out():
        @pl.loop(0, width // tile)
        def _(j):
            cols = pl.ds(pl.multiple_of(j * tile, tile), tile)
            back = lax.dot_general(pair_s[...], wgu[cols, :], across, preferred_element_type=F32)
            pb[:, cols] = back.astype(BF16)

    parts, from_core = (pm, pb), (cr_m, cr_b)
    to_x, from_x = (xs_m, xs_b), (xr_m, xr_b)
    to_z, from_z = (zs_m, zs_b), (zr_m, zr_b)

    def core_copy(t, other):
        src = parts[t].at[pl.ds(column(1 - x if other else x, 1 - c), quarter)]
        q = 1 if other else 0
        return (src, from_core[t].at[q], core_send.at[t, q], core_recv.at[t, q], sibling)

    def core_go(t, other):
        go(*core_copy(t, other))

    def core_wait(t, other):
        remote(*core_copy(t, other)).wait_recv()

    def core_rows(zz):
        return pl.ds(pl.multiple_of(zz * tok, tok), tok)

    def x_copy(t, zz):
        return (to_x[t].at[zz], from_x[t].at[zz], x_send.at[t, zz], x_recv.at[t, zz], partner)

    order = far + [z]

    def send_x(t):
        core_wait(t, True)
        for zz in order:
            own = parts[t][rows(1 - x, c, zz), :].astype(F32)
            to_x[t][zz] = (own + from_core[t][1, core_rows(zz), :].astype(F32)).astype(BF16)
            go(*x_copy(t, zz))

    def joined(t, zz):
        own = parts[t][rows(x, c, zz), :].astype(F32)
        return own + from_core[t][0, core_rows(zz), :].astype(F32) + from_x[t][zz].astype(F32)

    def send_z(t):
        core_wait(t, False)
        for zz in far:
            remote(*x_copy(t, zz)).wait_recv()
            to_z[t][zz] = joined(t, zz).astype(BF16)
            go(to_z[t].at[zz], from_z[t].at[z], z_send.at[t, zz], z_recv.at[t, z], zdev(zz))

    def finish(t):
        remote(*x_copy(t, z)).wait_recv()
        total = joined(t, z)
        for zz in near:
            remote(
                to_z[t].at[zz], from_z[t].at[zz], z_send.at[t, zz], z_recv.at[t, zz], zdev(zz)
            ).wait_recv()
            total = total + from_z[t][zz].astype(F32)
        return total

    own_go(0)
    for s in range(1, n):
        pass_z(0, s)
        if s == 1:
            own_go(1)
        if s == 2:
            pass_z(1, 1)
    pass_x(0, [z] + near)
    for s in range(min(2, n - 1), n):
        pass_z(1, s)
    load_gu.wait()
    load_d.wait()
    await_sibling(0, False)
    await_sibling(0, True)
    forward_hidden()
    pass_x(1, [z] + near)
    forward_out()
    core_go(0, True)
    core_go(0, False)
    await_sibling(1, False)
    await_sibling(1, True)
    backward_hidden()
    send_x(0)
    backward_out()
    core_go(1, True)
    core_go(1, False)
    send_z(0)
    send_x(1)
    mixed_ref[...] = finish(0).astype(mixed_ref.dtype)
    send_z(1)
    total = finish(1)
    grad_ref[...] = total[:, :width].astype(grad_ref.dtype)
    dots = total[:, width:]
    place = lax.broadcasted_iota(jnp.int32, (tok, top), 1)
    picked = jnp.zeros((tok, top), F32)
    for k in range(top):
        value = jnp.sum(jnp.where(ids[:, k : k + 1] == lane_expert, dots, 0.0), axis=1, keepdims=True)
        picked = picked + jnp.where(place == k, value, 0.0)
    gcomb_ref[...] = picked.T
    for copy in sends:
        copy.wait_send()
    for cond, copy in maybe:
        pl.when(cond)(copy.wait_send)


def dense_plan(tokens, cotangent, expert_ids, combine, w_gate_up, w_down):
    n = lax.axis_size("node")
    tok, width = tokens.shape
    top = expert_ids.shape[1]
    ff = w_down.shape[1]
    total = 4 * n * tok
    wide = width + LANES
    vmem = pl.BlockSpec(memory_space=pltpu.VMEM)
    hbm = pl.BlockSpec(memory_space=pl.ANY)
    dma = pltpu.SemaphoreType.DMA
    mixed, grads, dots = pl.pallas_call(
        functools.partial(dense_kernel, n),
        out_shape=(
            jax.ShapeDtypeStruct((tok, width), BF16),
            jax.ShapeDtypeStruct((tok, width), BF16),
            jax.ShapeDtypeStruct((top, tok), F32),
        ),
        in_specs=[hbm] * 6,
        out_specs=(vmem, vmem, vmem),
        scratch_shapes=[
            pltpu.VMEM((top, tok), jnp.int32),
            pltpu.VMEM((top, tok), F32),
            pltpu.VMEM((width, 2 * ff), BF16),
            pltpu.VMEM((ff, width), BF16),
            pltpu.VMEM((total, wide), BF16),
            pltpu.VMEM((total, width), BF16),
            pltpu.VMEM((total, width), BF16),
            pltpu.VMEM((total, wide), BF16),
            pltpu.VMEM((total, ff), F32),
            pltpu.VMEM((total, ff), F32),
            pltpu.VMEM((total, ff), BF16),
            pltpu.VMEM((total, 2 * ff), BF16),
            pltpu.VMEM((2, n * tok, width), BF16),
            pltpu.VMEM((2, n * tok, wide), BF16),
            pltpu.VMEM((n, tok, width), BF16),
            pltpu.VMEM((n, tok, wide), BF16),
            pltpu.VMEM((n, tok, width), BF16),
            pltpu.VMEM((n, tok, wide), BF16),
            pltpu.VMEM((n, tok, width), BF16),
            pltpu.VMEM((n, tok, wide), BF16),
            pltpu.VMEM((n, tok, width), BF16),
            pltpu.VMEM((n, tok, wide), BF16),
            dma((6,)),
            dma((2, n)),
            dma((2, 4, n)),
            dma((2, 4, n)),
            dma((2, 2)),
            dma((2, 2)),
            dma((2, n)),
            dma((2, n)),
            dma((2, n)),
            dma((2, n)),
        ],
        compiler_params=pltpu.CompilerParams(
            collective_id=0, has_side_effects=True, vmem_limit_bytes=62 * 1024 * 1024
        ),
    )(tokens, cotangent, expert_ids.T, combine.T, w_gate_up, w_down)
    return mixed, grads, dots.T


def choose_plan(tokens, cotangent, expert_ids, combine, w_gate_up, w_down):
    local_count = lax.axis_size("local")
    experts = lax.axis_size("node") * local_count
    tok_rows, top_count = expert_ids.shape
    capacity = max(2, 2 * tok_rows * top_count // experts)
    dense = capacity >= tok_rows and local_count == 4 and 2 * experts <= LANES and tok_rows % 16 == 0
    plan = dense_plan if dense else per_device
    return plan(tokens, cotangent, expert_ids, combine, w_gate_up, w_down)


def solution(mesh):
    placed = (
        P(("dp", "node", "local"), None),
        P(("dp", "node", "local"), None),
        P(("dp", "node", "local"), None),
        P(("dp", "node", "local"), None),
        P(("node", "local"), None, None),
        P(("node", "local"), None, None),
    )
    return jax.shard_map(
        choose_plan,
        mesh=mesh,
        in_specs=placed,
        out_specs=(
            P(("dp", "node", "local"), None),
            P(("dp", "node", "local"), None),
            P(("dp", "node", "local"), None),
        ),
        check_vma=False,
    )
```

```python
import functools

import jax
import jax.numpy as jnp
from jax import lax
from jax.experimental import pallas as pl
from jax.experimental.pallas import tpu as pltpu
from jax.sharding import PartitionSpec as P

MESH = pl.DeviceIdType.MESH
LANES = 128
F32 = jnp.float32
BF16 = jnp.bfloat16


def expert_forward(rows, w_gate_up, w_down):
    width = w_down.shape[0]
    projected = jnp.dot(rows, w_gate_up, preferred_element_type=jnp.float32)
    gate = projected[:, :width]
    upward = projected[:, width:]
    hidden = (gate * jax.nn.sigmoid(gate) * upward).astype(jnp.bfloat16)
    output = jnp.dot(hidden, w_down, preferred_element_type=jnp.float32).astype(jnp.bfloat16)
    return (output, gate, upward)


def expert_backward(grads, gate, upward, w_gate_up, w_down):
    grad_hidden = lax.dot_general(
        grads, w_down, (((1,), (1,)), ((), ())), preferred_element_type=jnp.float32
    )
    sigmoid = jax.nn.sigmoid(gate)
    grad_gate = grad_hidden * upward * sigmoid * (1.0 + gate * (1.0 - sigmoid))
    grad_up = grad_hidden * gate * sigmoid
    paired = jnp.concatenate([grad_gate, grad_up], axis=1).astype(jnp.bfloat16)
    back = lax.dot_general(
        paired, w_gate_up, (((1,), (1,)), ((), ())), preferred_element_type=jnp.float32
    )
    return back.astype(jnp.bfloat16)


def node_tables(ids_all, weights_all, node_here, node_count, local_count, capacity):
    rows_all, top_count = ids_all.shape
    tok_rows = rows_all // node_count
    experts = node_count * local_count
    per_source = ids_all.reshape(node_count, tok_rows * top_count)
    onehot = (per_source[:, :, None] == jnp.arange(experts, dtype=jnp.int32)[None, None, :]).astype(
        jnp.int32
    )
    before = jnp.cumsum(onehot, axis=1) - onehot
    ranks = jnp.sum(before * onehot, axis=2)
    source = jnp.arange(node_count, dtype=jnp.int32)[:, None]
    inside = per_source // local_count == node_here
    slots = per_source % local_count * (node_count * capacity) + source * capacity + ranks
    slots = jnp.where(inside, slots, -1).reshape(rows_all, top_count)
    matches = (
        slots[None, :, :]
        == jnp.arange(local_count * node_count * capacity, dtype=jnp.int32)[:, None, None]
    )
    placing = jnp.any(matches, axis=2).astype(jnp.bfloat16)
    slot_weight = jnp.sum(jnp.where(matches, weights_all[None, :, :], 0.0), axis=(1, 2))
    return (matches, placing, slot_weight)


def per_device(tokens, cotangent, expert_ids, combine, w_gate_up, w_down):
    node_count = lax.axis_size("node")
    local_count = lax.axis_size("local")
    experts = node_count * local_count
    tok_rows, top_count = expert_ids.shape
    width = tokens.shape[1]
    capacity = max(2, 2 * tok_rows * top_count // experts)
    gate_up_one = w_gate_up[0]
    down_one = w_down[0]
    route = jnp.concatenate([expert_ids.astype(jnp.float32), combine], axis=1)
    route_all = lax.all_gather(route, "node", axis=0, tiled=True)
    ids_all = route_all[:, :top_count].astype(jnp.int32)
    weights_all = route_all[:, top_count:]
    tokens_all, cot_all = (
        lax.all_gather(tokens, "node", axis=0, tiled=True),
        lax.all_gather(cotangent, "node", axis=0, tiled=True),
    )
    matches, placing, slot_weight = node_tables(
        ids_all, weights_all, lax.axis_index("node"), node_count, local_count, capacity
    )
    send_x = jnp.dot(placing, tokens_all, preferred_element_type=jnp.float32).astype(jnp.bfloat16)
    send_x = send_x.reshape(local_count, node_count * capacity, width)
    cot_rows = jnp.dot(placing, cot_all, preferred_element_type=jnp.float32)
    send_g = (cot_rows * slot_weight[:, None]).astype(jnp.bfloat16)
    send_g = send_g.reshape(local_count, node_count * capacity, width)
    arrived, arrived_grad = (
        lax.all_to_all(send_x, "local", split_axis=0, concat_axis=0, tiled=True),
        lax.all_to_all(send_g, "local", split_axis=0, concat_axis=0, tiled=True),
    )
    output, gate, upward = expert_forward(arrived.reshape(-1, width), gate_up_one, down_one)
    back = expert_backward(arrived_grad.reshape(-1, width), gate, upward, gate_up_one, down_one)
    output = output.reshape(local_count, node_count * capacity, width)
    back = back.reshape(local_count, node_count * capacity, width)
    came_back, back_home = (
        lax.all_to_all(output, "local", split_axis=0, concat_axis=0, tiled=True),
        lax.all_to_all(back, "local", split_axis=0, concat_axis=0, tiled=True),
    )
    flat_out = came_back.reshape(-1, width).astype(jnp.float32)
    flat_back = back_home.reshape(-1, width)
    gather_rows = placing.T
    mixed_part = jnp.dot(
        gather_rows.astype(jnp.float32),
        flat_out * slot_weight[:, None],
        precision=lax.Precision.HIGHEST,
    )
    back_part = jnp.dot(gather_rows, flat_back, preferred_element_type=jnp.float32)
    slot_dot = jnp.sum(cot_rows * flat_out, axis=1)
    combine_part = jnp.sum(jnp.where(matches, slot_dot[:, None, None], 0.0), axis=0)
    mixed, grad_tokens, grad_combine = (
        lax.psum_scatter(mixed_part, "node", scatter_dimension=0, tiled=True),
        lax.psum_scatter(back_part, "node", scatter_dimension=0, tiled=True),
        lax.psum_scatter(combine_part, "node", scatter_dimension=0, tiled=True),
    )
    return (mixed.astype(jnp.bfloat16), grad_tokens.astype(jnp.bfloat16), grad_combine)


def dense_kernel(
    n,
    tok_hbm,
    cot_hbm,
    ids_hbm,
    comb_hbm,
    gate_up_hbm,
    down_hbm,
    mixed_ref,
    grad_ref,
    gcomb_ref,
    ids_t,
    comb_t,
    wgu,
    wd,
    xs,
    cs,
    pm,
    pb,
    gate_s,
    up_s,
    hid_s,
    pair_s,
    cr_m,
    cr_b,
    xs_m,
    xs_b,
    xr_m,
    xr_b,
    zs_m,
    zs_b,
    zr_m,
    zr_b,
    w_sem,
    nd_send,
    ag_send,
    ag_recv,
    core_send,
    core_recv,
    x_send,
    x_recv,
    z_send,
    z_recv,
):
    tok, width = tok_hbm.shape
    top = ids_hbm.shape[0]
    ff = wd.shape[0]
    z = lax.axis_index("node")
    local = lax.axis_index("local")
    x, c = local // 2, local % 2
    experts = n * 4
    me = z * 4 + local
    half = 2 * n * tok
    quarter = n * tok

    partner = {"local": (1 - x) * 2 + c}
    sibling = {"local": x * 2 + 1 - c}

    reach = jnp.minimum(z, n - 1 - z)
    toward = jnp.where(z < n - 1 - z, 1, -1)
    near = []
    for s in range(1, n):
        turn = (s + 1) // 2 * (1 if s % 2 else -1)
        near.append(z + toward * jnp.where(s <= 2 * reach, turn, s - reach))
    far = near[::-1]

    def zdev(zz):
        return {"node": zz}

    def column(xx, cc):
        return pl.multiple_of((xx * 2 + cc) * quarter, quarter)

    def rows(xx, cc, zz):
        return pl.ds(pl.multiple_of(((xx * 2 + cc) * n + zz) * tok, tok), tok)

    mine = rows(x, c, z)
    load_own = [
        pltpu.make_async_copy(ids_hbm, ids_t, w_sem.at[2]),
        pltpu.make_async_copy(comb_hbm, comb_t, w_sem.at[3]),
        pltpu.make_async_copy(tok_hbm, xs.at[mine, pl.ds(0, width)], w_sem.at[4]),
        pltpu.make_async_copy(cot_hbm, cs.at[mine], w_sem.at[5]),
    ]
    for copy in load_own:
        copy.start()
    load_gu = pltpu.make_async_copy(gate_up_hbm.at[0], wgu, w_sem.at[0])
    load_d = pltpu.make_async_copy(down_hbm.at[0], wd, w_sem.at[1])
    load_gu.start()
    load_d.start()

    barrier = pltpu.get_barrier_semaphore()
    for zz in near:
        pl.semaphore_signal(barrier, inc=1, device_id=zdev(zz), device_id_type=MESH)
    pl.semaphore_signal(barrier, inc=1, device_id=partner, device_id_type=MESH)
    pl.semaphore_signal(barrier, inc=1, device_id=sibling, device_id_type=MESH)

    for copy in load_own:
        copy.wait()
    lane = lax.broadcasted_iota(jnp.int32, (tok, LANES), 1)
    lane_expert = jnp.where(lane < experts, lane, lane - experts)
    ids = ids_t[...].T
    comb = comb_t[...].T
    weight = jnp.zeros((tok, LANES), F32)
    for k in range(top):
        weight = weight + jnp.where(ids[:, k : k + 1] == lane_expert, comb[:, k : k + 1], 0.0)
    coarse = weight.astype(BF16).astype(F32)
    xs[mine, width:] = jnp.where(lane < experts, coarse, weight - coarse).astype(BF16)
    pl.semaphore_wait(barrier, n + 1)

    sends = []
    maybe = []

    def remote(src, dst, send_sem, recv_sem, device):
        return pltpu.make_async_remote_copy(
            src_ref=src,
            dst_ref=dst,
            send_sem=send_sem,
            recv_sem=recv_sem,
            device_id=device,
            device_id_type=MESH,
        )

    def go(*args):
        copy = remote(*args)
        copy.start()
        sends.append(copy)

    bufs = (xs, cs)

    def gather_go(t, role, zz, where, device):
        go(bufs[t].at[where], bufs[t].at[where], ag_send.at[t, role, zz], ag_recv.at[t, role, zz], device)

    def gather_wait(t, role, zz, where):
        remote(
            bufs[t].at[where], bufs[t].at[where], ag_send.at[t, role, zz], ag_recv.at[t, role, zz], sibling
        ).wait_recv()

    def inside(zz):
        return (zz >= 0) & (zz < n)

    def go_if(cond, *args):
        copy = remote(*args)
        pl.when(cond)(copy.start)
        maybe.append((cond, copy))

    def own_go(t):
        for i, to in enumerate((z - 1, z + 1)):
            device = zdev(jnp.clip(to, 0, n - 1))
            block = bufs[t].at[mine]
            go_if(inside(to), block, block, nd_send.at[t, i], ag_recv.at[t, 0, z], device)
        gather_go(t, 1, z, mine, partner)
        gather_go(t, 2, z, mine, sibling)

    def pass_z(t, s):
        for side in (-1, 1):
            here = inside(z + side * s)
            zz = jnp.clip(z + side * s, 0, n - 1)
            to = z - side
            where = rows(x, c, zz)
            block = bufs[t].at[where]
            pl.when(here)(functools.partial(gather_wait, t, 0, zz, where))
            if s < n - 1:
                device = zdev(jnp.clip(to, 0, n - 1))
                go_if(here & inside(to), block, block, ag_send.at[t, 0, zz], ag_recv.at[t, 0, zz], device)
            go_if(here, block, block, ag_send.at[t, 1, zz], ag_recv.at[t, 1, zz], partner)
            go_if(here, block, block, ag_send.at[t, 2, zz], ag_recv.at[t, 2, zz], sibling)

    def pass_x(t, places):
        for zz in places:
            where = rows(1 - x, c, zz)
            gather_wait(t, 1, zz, where)
            gather_go(t, 3, zz, where, sibling)

    def await_sibling(t, other):
        for zz in [z] + near:
            where = rows(1 - x if other else x, 1 - c, zz)
            gather_wait(t, 3 if other else 2, zz, where)

    tile = 512 if width % 512 == 0 else width
    total_rows = 2 * half
    wide_lane = lax.broadcasted_iota(jnp.int32, (total_rows, LANES), 1)

    def my_weight():
        block = xs[:, width:].astype(F32)
        chosen = (wide_lane == me) | (wide_lane == me + experts)
        return jnp.sum(jnp.where(chosen, block, 0.0), axis=1, keepdims=True)

    def forward():
        projected = jnp.dot(xs[:, :width], wgu[...], preferred_element_type=F32)
        gate = projected[:, :ff]
        upward = projected[:, ff:]
        hidden = (gate * jax.nn.sigmoid(gate) * upward).astype(BF16)
        gate_s[...] = gate
        up_s[...] = upward
        hid_s[...] = hidden
        weight = my_weight()

        @pl.loop(0, width // tile)
        def _(j):
            cols = pl.ds(pl.multiple_of(j * tile, tile), tile)
            out = jnp.dot(hid_s[...], wd[:, cols], preferred_element_type=F32)
            pm[:, cols] = (out * weight).astype(BF16)

    across = (((1,), (1,)), ((), ()))

    def backward():
        plain = lax.dot_general(cs[...], wd[...], across, preferred_element_type=F32)
        gate = gate_s[...]
        upward = up_s[...]
        grads = plain * my_weight()
        sig = jax.nn.sigmoid(gate)
        grad_gate = grads * upward * sig * (1.0 + gate * (1.0 - sig))
        grad_up = grads * gate * sig
        dots = jnp.sum(plain * hid_s[...].astype(F32), axis=1, keepdims=True)
        coarse = dots.astype(BF16).astype(F32)
        pb[:, width:] = jnp.where(
            wide_lane == me, coarse, jnp.where(wide_lane == me + experts, dots - coarse, 0.0)
        ).astype(BF16)
        pair_s[:, :ff] = grad_gate.astype(BF16)
        pair_s[:, ff:] = grad_up.astype(BF16)

        @pl.loop(0, width // tile)
        def _(j):
            cols = pl.ds(pl.multiple_of(j * tile, tile), tile)
            back = lax.dot_general(pair_s[...], wgu[cols, :], across, preferred_element_type=F32)
            pb[:, cols] = back.astype(BF16)

    parts, from_core = (pm, pb), (cr_m, cr_b)
    to_x, from_x = (xs_m, xs_b), (xr_m, xr_b)
    to_z, from_z = (zs_m, zs_b), (zr_m, zr_b)

    def core_copy(t, other):
        src = parts[t].at[pl.ds(column(1 - x if other else x, 1 - c), quarter)]
        q = 1 if other else 0
        return (src, from_core[t].at[q], core_send.at[t, q], core_recv.at[t, q], sibling)

    def core_go(t, other):
        go(*core_copy(t, other))

    def core_wait(t, other):
        remote(*core_copy(t, other)).wait_recv()

    def core_rows(zz):
        return pl.ds(pl.multiple_of(zz * tok, tok), tok)

    def x_copy(t, zz):
        return (to_x[t].at[zz], from_x[t].at[zz], x_send.at[t, zz], x_recv.at[t, zz], partner)

    order = far + [z]

    def send_x(t):
        core_wait(t, True)
        for zz in order:
            own = parts[t][rows(1 - x, c, zz), :].astype(F32)
            to_x[t][zz] = (own + from_core[t][1, core_rows(zz), :].astype(F32)).astype(BF16)
            go(*x_copy(t, zz))

    def joined(t, zz):
        own = parts[t][rows(x, c, zz), :].astype(F32)
        return own + from_core[t][0, core_rows(zz), :].astype(F32) + from_x[t][zz].astype(F32)

    def send_z(t):
        core_wait(t, False)
        for zz in far:
            remote(*x_copy(t, zz)).wait_recv()
            to_z[t][zz] = joined(t, zz).astype(BF16)
            go(to_z[t].at[zz], from_z[t].at[z], z_send.at[t, zz], z_recv.at[t, z], zdev(zz))

    def finish(t):
        remote(*x_copy(t, z)).wait_recv()
        total = joined(t, z)
        for zz in near:
            remote(
                to_z[t].at[zz], from_z[t].at[zz], z_send.at[t, zz], z_recv.at[t, zz], zdev(zz)
            ).wait_recv()
            total = total + from_z[t][zz].astype(F32)
        return total

    own_go(0)
    for s in range(1, n):
        pass_z(0, s)
        if s == 1:
            own_go(1)
        if s == 2:
            pass_z(1, 1)
    pass_x(0, [z] + near)
    for s in range(min(2, n - 1), n):
        pass_z(1, s)
    load_gu.wait()
    load_d.wait()
    await_sibling(0, False)
    await_sibling(0, True)
    forward()
    core_go(0, True)
    core_go(0, False)
    pass_x(1, [z] + near[:1])
    send_x(0)
    pass_x(1, near[1:])
    await_sibling(1, False)
    await_sibling(1, True)
    backward()
    core_go(1, True)
    core_go(1, False)
    send_z(0)
    send_x(1)
    mixed_ref[...] = finish(0).astype(mixed_ref.dtype)
    send_z(1)
    total = finish(1)
    grad_ref[...] = total[:, :width].astype(grad_ref.dtype)
    dots = total[:, width:]
    place = lax.broadcasted_iota(jnp.int32, (tok, top), 1)
    picked = jnp.zeros((tok, top), F32)
    for k in range(top):
        value = jnp.sum(jnp.where(ids[:, k : k + 1] == lane_expert, dots, 0.0), axis=1, keepdims=True)
        picked = picked + jnp.where(place == k, value, 0.0)
    gcomb_ref[...] = picked.T
    for copy in sends:
        copy.wait_send()
    for cond, copy in maybe:
        pl.when(cond)(copy.wait_send)


def dense_plan(tokens, cotangent, expert_ids, combine, w_gate_up, w_down):
    n = lax.axis_size("node")
    tok, width = tokens.shape
    top = expert_ids.shape[1]
    ff = w_down.shape[1]
    total = 4 * n * tok
    wide = width + LANES
    vmem = pl.BlockSpec(memory_space=pltpu.VMEM)
    hbm = pl.BlockSpec(memory_space=pl.ANY)
    dma = pltpu.SemaphoreType.DMA
    mixed, grads, dots = pl.pallas_call(
        functools.partial(dense_kernel, n),
        out_shape=(
            jax.ShapeDtypeStruct((tok, width), BF16),
            jax.ShapeDtypeStruct((tok, width), BF16),
            jax.ShapeDtypeStruct((top, tok), F32),
        ),
        in_specs=[hbm] * 6,
        out_specs=(vmem, vmem, vmem),
        scratch_shapes=[
            pltpu.VMEM((top, tok), jnp.int32),
            pltpu.VMEM((top, tok), F32),
            pltpu.VMEM((width, 2 * ff), BF16),
            pltpu.VMEM((ff, width), BF16),
            pltpu.VMEM((total, wide), BF16),
            pltpu.VMEM((total, width), BF16),
            pltpu.VMEM((total, width), BF16),
            pltpu.VMEM((total, wide), BF16),
            pltpu.VMEM((total, ff), F32),
            pltpu.VMEM((total, ff), F32),
            pltpu.VMEM((total, ff), BF16),
            pltpu.VMEM((total, 2 * ff), BF16),
            pltpu.VMEM((2, n * tok, width), BF16),
            pltpu.VMEM((2, n * tok, wide), BF16),
            pltpu.VMEM((n, tok, width), BF16),
            pltpu.VMEM((n, tok, wide), BF16),
            pltpu.VMEM((n, tok, width), BF16),
            pltpu.VMEM((n, tok, wide), BF16),
            pltpu.VMEM((n, tok, width), BF16),
            pltpu.VMEM((n, tok, wide), BF16),
            pltpu.VMEM((n, tok, width), BF16),
            pltpu.VMEM((n, tok, wide), BF16),
            dma((6,)),
            dma((2, n)),
            dma((2, 4, n)),
            dma((2, 4, n)),
            dma((2, 2)),
            dma((2, 2)),
            dma((2, n)),
            dma((2, n)),
            dma((2, n)),
            dma((2, n)),
        ],
        compiler_params=pltpu.CompilerParams(
            collective_id=0, has_side_effects=True, vmem_limit_bytes=62 * 1024 * 1024
        ),
    )(tokens, cotangent, expert_ids.T, combine.T, w_gate_up, w_down)
    return mixed, grads, dots.T


def choose_plan(tokens, cotangent, expert_ids, combine, w_gate_up, w_down):
    local_count = lax.axis_size("local")
    experts = lax.axis_size("node") * local_count
    tok_rows, top_count = expert_ids.shape
    capacity = max(2, 2 * tok_rows * top_count // experts)
    dense = capacity >= tok_rows and local_count == 4 and 2 * experts <= LANES and tok_rows % 16 == 0
    plan = dense_plan if dense else per_device
    return plan(tokens, cotangent, expert_ids, combine, w_gate_up, w_down)


def solution(mesh):
    placed = (
        P(("dp", "node", "local"), None),
        P(("dp", "node", "local"), None),
        P(("dp", "node", "local"), None),
        P(("dp", "node", "local"), None),
        P(("node", "local"), None, None),
        P(("node", "local"), None, None),
    )
    return jax.shard_map(
        choose_plan,
        mesh=mesh,
        in_specs=placed,
        out_specs=(
            P(("dp", "node", "local"), None),
            P(("dp", "node", "local"), None),
            P(("dp", "node", "local"), None),
        ),
        check_vma=False,
    )
```
